32 devices in a mesh: ctx: 8 (over z, x), tp: 4 (over y, core).
Axes of the slice: x: 2, y: 2, z: 4, core: 2. Of those that a mesh axis runs over, the one named last changes fastest.
Arguments:
- query: bfloat16 [1024, 8192], P('ctx', 'tp'), may hold values from -6 to 6
- keys: bfloat16 [1024, 8192], P('ctx', 'tp'), may hold values from -6 to 6
- values: bfloat16 [1024, 8192], P('ctx', 'tp'), may hold values from -6 to 6
- rates: float32 [16, 8192], P(None, 'tp'), may hold values from 0.00048828125 to 0.03
- residues: float32 [16, 8192], P(None, 'tp'), may hold values from -3 to 3
- skip: float32 [8192], P('tp'), may hold values from 0.25 to 1.5
- gain: float32 [8192], P('tp'), may hold values from 0.25 to 1.75
Outputs:
- mixed: bfloat16 [1024, 8192], P('ctx', 'tp')
The draws below stay inside these ranges and needn't reach their ends.
All inputs are finite; a program needn't handle non-finite values.
Results may differ from the reference program's by a relative error of at most 0.0025.
Values sent between devices are 32-bit elements; how exact they have to be, the bound alone decides.
No kernel may reach another device: no remote copies, remote signals or barrier semaphores. Data moves between devices by JAX's collectives and lax.ppermute only.
A program may use at most 64 MiB of HBM per device.

```python
import math
import jax
import jax.numpy as jnp
from jax import lax

C = 8192
M = 16
TOKENS = 1024


def block_levels(key, shape, shards, least, largest):
    def one(position, shards_of):
        steps = jax.random.uniform(jax.random.fold_in(jax.random.fold_in(key, 6), position), (shards_of,), jnp.float32, least / len(shards), largest / len(shards))
        return jnp.repeat(jnp.exp(steps), shape[position] // shards_of).reshape((-1,) + (1,) * (len(shape) - position - 1))

    loudness = one(*shards[0])
    for cut in shards[1:]:
        loudness = loudness * one(*cut)
    return loudness


def noise(rng, shape, scale, most, cuts=(), kind=jnp.bfloat16):
    drawn = jax.random.normal(rng, shape, jnp.float32) * scale
    if len(cuts) > 0:
        drawn = block_levels(rng, shape, cuts, -0.22, 0.18) * drawn
    return jnp.clip(drawn, min=-most, max=most).astype(kind)


def setup_inputs(seed: int = 0) -> dict:
    streams_of = jax.random.split(jax.random.key(seed), 8)
    return {
        "query": noise(streams_of[0], (TOKENS, C), 1.0, 6.0, ((0, 8), (1, 4))),
        "keys": noise(streams_of[1], (TOKENS, C), 1.0, 6.0, ((0, 8), (1, 4))),
        "values": noise(streams_of[2], (TOKENS, C), 1.0, 6.0, ((0, 8), (1, 4))),
        "rates": jnp.clip(jnp.exp(math.log(0.03) - 4.118061 * jax.random.uniform(streams_of[3], (M, C), jnp.float32) ** block_levels(streams_of[3], (M, C), ((1, 4),), -0.2, 0.2)), 0.00048828125, 0.03),
        "residues": noise(streams_of[4], (M, C), 0.5, 3.0, ((1, 4),), jnp.float32),
        "skip": jnp.clip(0.25 + 1.25 * jax.random.uniform(streams_of[5], (C,), jnp.float32) ** block_levels(streams_of[5], (C,), ((0, 4),), -0.2, 0.2), 0.25, 1.5),
        "gain": jnp.clip(1.0 + 0.15 * jax.random.normal(streams_of[6], (C,), jnp.float32), 0.25, 1.75),
    }


def combine_pair(first, second):
    return (first[0] * second[0], first[1] * second[0] + second[1])

def channel_block(items):
    driven, rates, residues = items

    def one_mode(total, mode):
        rate, residue = mode
        decay = jnp.exp(-rate)
        scale = residue * jnp.sqrt(1.0 - decay * decay)
        factors = jnp.broadcast_to(decay[None, :], driven.shape)
        state = lax.associative_scan(combine_pair, (factors, driven), axis=0)[1]
        return (total + scale[None, :] * state, None)
    start = jnp.zeros(driven.shape, jnp.float32)
    total, unused = lax.scan(one_mode, start, (rates, residues))
    return total

def reference(query, keys, values, rates, residues, skip, gain):
    driven = keys.astype(jnp.float32) * values.astype(jnp.float32)
    width = min(C, 1024)
    blocks = C // width
    driven_blocks = driven.reshape(TOKENS, blocks, width).transpose(1, 0, 2)
    rate_blocks = rates.reshape(M, blocks, width).transpose(1, 0, 2)
    residue_blocks = residues.reshape(M, blocks, width).transpose(1, 0, 2)
    filtered = lax.map(channel_block, (driven_blocks, rate_blocks, residue_blocks))
    filtered = filtered.transpose(1, 0, 2).reshape(TOKENS, C)
    gated = query.astype(jnp.float32) * (filtered + skip[None, :] * driven)
    power = lax.optimization_barrier(jnp.mean(gated * gated, axis=1))
    return (gated * lax.rsqrt(power + 1e-06)[:, None] * gain[None, :]).astype(jnp.bfloat16)
```

```python
import jax
import jax.numpy as jnp
from jax import lax
from jax.experimental import pallas as pl
from jax.experimental.pallas import tpu as pltpu
from jax.sharding import PartitionSpec as P

C = 8192
LANES = 128
ROWS = 8
F32 = jnp.float32


def lanes(group):
    return pl.ds(pl.multiple_of(group * LANES, LANES), LANES)


def own_half_first(x_ref, source, ordered):
    half = source.shape[0] // 2
    first = pl.multiple_of(x_ref[0] * half, half)
    ordered[:half, :] = source[pl.ds(first, half), :]
    ordered[half:, :] = source[pl.ds(pl.multiple_of(half - first, half), half), :]


def end_states_kernel(modes, x_ref, keys, values, rates, mine, other, ordered):
    count, width = keys.shape
    half = modes // 2
    own_half_first(x_ref, rates, ordered)
    below = (ROWS - 1 - lax.broadcasted_iota(jnp.int32, (ROWS, LANES), 0)).astype(F32)

    def group_step(group, unused):
        at = lanes(group)
        driven = keys[:, at].astype(F32) * values[:, at].astype(F32)
        blocks = [driven[i:i + ROWS] for i in range(0, count, ROWS)]
        for start, out in ((0, mine), (half, other)):
            for mode in range(half):
                rate = jnp.broadcast_to(ordered[start + mode:start + mode + 1, at], (ROWS, LANES))
                factor = jnp.exp(-ROWS * rate)
                state = blocks[0]
                for block in blocks[1:]:
                    state = state * factor + block
                state = state * jnp.exp(-rate * below)
                out[mode:mode + 1, at] = jnp.sum(state, axis=0, keepdims=True)
        return unused

    lax.fori_loop(0, width // LANES, group_step, 0)


def local_kernel(modes, query, keys, values, rates, residues, skip, out, series, rate_rows, scale_rows):
    count, width = keys.shape
    groups = width // LANES

    def spread_params(group, unused):
        at = lanes(group)
        for i in range(0, modes, ROWS):
            rows = pl.ds(i * groups + group, ROWS, stride=groups)
            decay = jnp.exp(-rates[i:i + ROWS, at])
            rate_rows[rows, :] = decay
            scale_rows[rows, :] = residues[i:i + ROWS, at] * jnp.sqrt(1.0 - decay * decay)
        return unused

    lax.fori_loop(0, groups, spread_params, 0)

    def spread(group, unused):
        at = lanes(group)
        driven = keys[:, at].astype(F32) * values[:, at].astype(F32)
        for i in range(0, count, ROWS):
            series[pl.ds(i * groups + group, ROWS, stride=groups), :] = driven[i:i + ROWS]
        return unused

    lax.fori_loop(0, groups, spread, 0)

    for part in range(0, groups, ROWS):
        decays = [rate_rows[m * groups + part:m * groups + part + ROWS, :] for m in range(modes)]
        scales = [scale_rows[m * groups + part:m * groups + part + ROWS, :] for m in range(modes)]

        def token(t, states):
            rows = pl.ds(pl.multiple_of(t * groups + part, ROWS), ROWS)
            now = series[rows, :]
            states = [s * d + now for s, d in zip(states, decays)]
            terms = [s * w for s, w in zip(states, scales)]
            while len(terms) > 1:
                terms = [a + b for a, b in zip(terms[::2], terms[1::2])]
            series[rows, :] = terms[0]
            return states

        lax.fori_loop(0, count, token, [jnp.zeros((ROWS, LANES), F32)] * modes, unroll=2)

    def gate(group, unused):
        at = lanes(group)
        driven = keys[:, at].astype(F32) * values[:, at].astype(F32)
        gates = query[:, at].astype(F32)
        through = skip[:, at]
        for i in range(0, count, ROWS):
            filtered = series[pl.ds(i * groups + group, ROWS, stride=groups), :]
            out[i:i + ROWS, at] = gates[i:i + ROWS] * (filtered + through * driven[i:i + ROWS])
        return unused

    lax.fori_loop(0, groups, gate, 0)


def carry_kernel(modes, x_ref, local, query, kept, received, rates, residues, gated, squares, sums, ordered, weights):
    count, width = query.shape
    half = modes // 2
    own_half_first(x_ref, rates, ordered)
    own_half_first(x_ref, residues, weights)
    decay = jnp.exp(-ordered[...])
    weights[...] = weights[...] * jnp.sqrt(1.0 - decay * decay)
    weights[:half, :] *= kept[...]
    weights[half:, :] *= received[...]
    ahead = (1 + lax.broadcasted_iota(jnp.int32, (ROWS, LANES), 0)).astype(F32)
    sums[...] = jnp.zeros_like(sums)

    def group_step(group, unused):
        at = lanes(group)
        gates = query[:, at].astype(F32)
        terms, factors = [], []
        for mode in range(modes):
            rate = jnp.broadcast_to(ordered[mode:mode + 1, at], (ROWS, LANES))
            weight = jnp.broadcast_to(weights[mode:mode + 1, at], (ROWS, LANES))
            terms.append(weight * jnp.exp(-rate * ahead))
            factors.append(jnp.exp(-ROWS * rate))
        for i in range(0, count, ROWS):
            total = terms
            while len(total) > 1:
                total = [a + b for a, b in zip(total[::2], total[1::2])]
            result = local[i:i + ROWS, at] + gates[i:i + ROWS] * total[0]
            gated[i:i + ROWS, at] = result
            sums[i:i + ROWS, :] += result * result
            if i + ROWS < count:
                terms = [t * f for t, f in zip(terms, factors)]
        return unused

    lax.fori_loop(0, width // LANES, group_step, 0)
    squares[...] = jnp.sum(jnp.transpose(sums[...]), axis=0, keepdims=True)


def norm_kernel(gated, gain, *rest):
    *parts, out = rest
    count, width = gated.shape
    total = parts[0][...]
    for part in parts[1:]:
        total = total + part[...]
    factor = lax.rsqrt(total / C + 1e-06)
    factor = jnp.transpose(jnp.broadcast_to(factor, (count, count)))[:, :LANES]

    def group_step(group, unused):
        at = lanes(group)
        out[:, at] = (gated[:, at] * factor * gain[:, at]).astype(out.dtype)
        return unused

    lax.fori_loop(0, width // LANES, group_step, 0)


VMEM = pl.BlockSpec(memory_space=pltpu.VMEM)
SMEM = pl.BlockSpec(memory_space=pltpu.SMEM)


def call(kernel, inputs, outputs, scratch=(), scalar=False, flops=0, name=None):
    size = sum(x.size * x.dtype.itemsize for x in (*inputs, *outputs))
    return pl.pallas_call(
        kernel,
        out_shape=outputs,
        in_specs=[SMEM if scalar and i == 0 else VMEM for i in range(len(inputs))],
        out_specs=[VMEM] * len(outputs),
        scratch_shapes=scratch,
        cost_estimate=pl.CostEstimate(flops=flops, bytes_accessed=size, transcendentals=0),
        compiler_params=pltpu.CompilerParams(vmem_limit_bytes=32 * 1024 * 1024),
        name=name,
    )(*inputs)


def body(ctx, tp, query, keys, values, rates, residues, skip, gain):
    count, width = keys.shape
    modes = rates.shape[0]
    half = modes // 2
    outer = ctx // 2
    f32 = lambda *shape: jax.ShapeDtypeStruct(shape, F32)
    own = lax.axis_index("ctx").astype(jnp.int32)
    z, x = own // 2, own % 2
    x_ref = x.reshape(1)

    mine, other = call(
        lambda *refs: end_states_kernel(modes, *refs),
        (x_ref, keys, values, rates),
        (f32(half, width), f32(half, width)),
        scratch=[pltpu.VMEM((modes, width), F32)],
        scalar=True,
        flops=2 * modes * count * width,
        name="end_states",
    )
    (local,) = call(
        lambda *refs: local_kernel(modes, *refs),
        (query, keys, values, rates, residues, skip[None]),
        (f32(count, width),),
        scratch=[
            pltpu.VMEM((count * width // LANES, LANES), F32),
            pltpu.VMEM((modes * width // LANES, LANES), F32),
            pltpu.VMEM((modes * width // LANES, LANES), F32),
        ],
        flops=4 * modes * count * width,
        name="local_filter",
    )

    pair = [(i, i ^ 1) for i in range(ctx)]

    def shifted(array, by):
        return lax.ppermute(array, "ctx", [(i, (i + 2 * by) % ctx) for i in range(ctx)])

    my_rates = jnp.where(x == 0, rates[:half], rates[half:])
    step = jnp.exp(-my_rates * count)
    partner = lax.ppermute(other, "ctx", pair)
    pair_state = jnp.where(x == 0, mine * step + partner, partner * step + mine)

    span = min(3, outer - 1)
    before = jnp.zeros_like(mine)
    for by, moved in [(by, shifted(pair_state, by)) for by in range(span, 0, -1)]:
        weight = jnp.exp(-my_rates * (2 * count * (by - 1)))
        before = before + jnp.where(z >= by, weight * moved, 0.0)
    while span < outer - 1:
        moves = [(by, shifted(before, by)) for by in range(3 * span, 0, -span) if by < outer]
        for by, moved in moves:
            weight = jnp.exp(-my_rates * (2 * count * by))
            before = before + jnp.where(z >= by, weight * moved, 0.0)
        span = 4 * span

    second = before * step + jnp.where(x == 0, mine, partner)
    kept = jnp.where(x == 0, before, second)
    received = lax.ppermute(jnp.where(x == 0, second, before), "ctx", pair)

    gated, squares = call(
        lambda *refs: carry_kernel(modes, *refs),
        (x_ref, local, query, kept, received, rates, residues),
        (f32(count, width), f32(1, count)),
        scratch=[
            pltpu.VMEM((count, LANES), F32),
            pltpu.VMEM((modes, width), F32),
            pltpu.VMEM((modes, width), F32),
        ],
        scalar=True,
        flops=2 * modes * count * width,
        name="add_carry",
    )
    parts = [squares] + [
        lax.ppermute(squares, "tp", [(i, (i + by) % tp) for i in range(tp)]) for by in range(1, tp)
    ]
    (out,) = call(
        norm_kernel,
        (gated, gain[None], *parts),
        (jax.ShapeDtypeStruct((count, width), jnp.bfloat16),),
        flops=2 * count * width,
        name="norm",
    )
    return out


def solution(mesh):
    ctx, tp = mesh.shape["ctx"], mesh.shape["tp"]
    in_specs = (
        P("ctx", "tp"),
        P("ctx", "tp"),
        P("ctx", "tp"),
        P(None, "tp"),
        P(None, "tp"),
        P("tp"),
        P("tp"),
    )
    return jax.shard_map(
        lambda *arrays: body(ctx, tp, *arrays),
        mesh=mesh,
        in_specs=in_specs,
        out_specs=P("ctx", "tp"),
        check_vma=False,
    )
```

```python
import jax
import jax.numpy as jnp
from jax import lax
from jax.experimental import pallas as pl
from jax.experimental.pallas import tpu as pltpu
from jax.sharding import PartitionSpec as P

C = 8192
LANES = 128
ROWS = 8
F32 = jnp.float32
VMEM = pl.BlockSpec(memory_space=pltpu.VMEM)
SMEM = pl.BlockSpec(memory_space=pltpu.SMEM)
HBM = pl.BlockSpec(memory_space=pltpu.HBM)


def lanes(group):
    return pl.ds(pl.multiple_of(group * LANES, LANES), LANES)


def added(terms):
    terms = list(terms)
    while len(terms) > 1:
        terms = [a + b for a, b in zip(terms[::2], terms[1::2])]
    return terms[0]


def spread_row(ref, row, at):
    return jnp.broadcast_to(ref[row:row + 1, at], (ROWS, LANES))


def end_states(blocks, decay, decay8, decay16, turn, out, at):
    modes = decay.shape[0]
    for mode in range(modes):
        factor = spread_row(decay16, mode, at)
        even, odd = blocks[0], blocks[1]
        for i in range(2, len(blocks), 2):
            even = even * factor + blocks[i]
            odd = odd * factor + blocks[i + 1]
        turn[mode * ROWS:(mode + 1) * ROWS, :] = even * spread_row(decay8, mode, at) + odd
    step = decay[:, at]
    state = turn[pl.ds(0, modes, stride=ROWS), :]
    for token in range(1, ROWS):
        state = state * step + turn[pl.ds(token, modes, stride=ROWS), :]
    out[:, at] = state


def set_decays(rate, decay, decay8, decay16):
    decay[...] = jnp.exp(-rate)
    decay8[...] = jnp.exp(-ROWS * rate)
    decay16[...] = jnp.exp(-2 * ROWS * rate)


def first_ends_kernel(chunks, x_ref, keys, values, rates, other, driven, key_buf, value_buf, rate_buf,
                      decay, decay8, decay16, turn, sems):
    count, width = key_buf.shape
    half = rate_buf.shape[0]
    size = width // chunks
    start = pl.multiple_of((1 - x_ref[0]) * half, half)
    rate_copy = pltpu.make_async_copy(rates.at[pl.ds(start, half), :], rate_buf, sems.at[2 * chunks])
    rate_copy.start()
    copies = []
    for i in range(chunks):
        at = pl.ds(i * size, size)
        for j, (source, target) in enumerate(((keys, key_buf), (values, value_buf))):
            copies.append(pltpu.make_async_copy(source.at[:, at], target.at[:, at], sems.at[2 * i + j]))
            copies[-1].start()
    rate_copy.wait()
    set_decays(rate_buf[...], decay, decay8, decay16)

    def group_step(group, unused):
        at = lanes(group)
        product = key_buf[:, at].astype(F32) * value_buf[:, at].astype(F32)
        driven[:, at] = product
        blocks = [product[i:i + ROWS] for i in range(0, count, ROWS)]
        end_states(blocks, decay, decay8, decay16, turn.at[group % 2], other, at)
        return unused

    groups = size // LANES
    for i in range(chunks):
        copies[2 * i].wait()
        copies[2 * i + 1].wait()
        lax.fori_loop(i * groups, (i + 1) * groups, group_step, 0, unroll=min(2, groups))


def second_ends_kernel(x_ref, driven, rates, mine, decay, decay8, decay16, turn):
    count, width = driven.shape
    half = rates.shape[0] // 2
    set_decays(rates[pl.ds(pl.multiple_of(x_ref[0] * half, half), half), :], decay, decay8, decay16)

    def group_step(group, unused):
        at = lanes(group)
        blocks = [driven[i:i + ROWS, at] for i in range(0, count, ROWS)]
        end_states(blocks, decay, decay8, decay16, turn.at[group % 2], mine, at)
        return unused

    lax.fori_loop(0, width // LANES, group_step, 0, unroll=2)


def local_kernel(part, query, driven, rates, residues, skip, out, series, decays, scales):
    count = driven.shape[0]
    modes = rates.shape[0]

    def spread(i, unused):
        here = lanes(i)
        at = lanes(part * ROWS + i)
        for mode in range(0, modes, ROWS):
            rows = pl.ds(mode * ROWS + i, ROWS, stride=ROWS)
            decay = jnp.exp(-rates[mode:mode + ROWS, at])
            decays[rows, :] = decay
            scales[rows, :] = residues[mode:mode + ROWS, at] * jnp.sqrt(1.0 - decay * decay)
        for token in range(0, count, ROWS):
            series[pl.ds(token * ROWS + i, ROWS, stride=ROWS), :] = driven[token:token + ROWS, at]
        return unused

    lax.fori_loop(0, ROWS, spread, 0, unroll=2)
    decay = [decays[m * ROWS:(m + 1) * ROWS, :] for m in range(modes)]
    scale = [scales[m * ROWS:(m + 1) * ROWS, :] for m in range(modes)]

    def token_step(token, states):
        rows = pl.ds(pl.multiple_of(token * ROWS, ROWS), ROWS)
        now = series[rows, :]
        states = [s * d + now for s, d in zip(states, decay)]
        series[rows, :] = added(s * w for s, w in zip(states, scale))
        return states

    lax.fori_loop(0, count, token_step, [jnp.zeros((ROWS, LANES), F32)] * modes, unroll=8)

    def gate(i, unused):
        here = lanes(i)
        at = lanes(part * ROWS + i)
        gates = query[:, at].astype(F32)
        for token in range(0, count, ROWS):
            filtered = series[pl.ds(token * ROWS + i, ROWS, stride=ROWS), :]
            out[token:token + ROWS, here] = gates[token:token + ROWS] * (
                filtered + skip[:, at] * driven[token:token + ROWS, at]
            )
        return unused

    lax.fori_loop(0, ROWS, gate, 0, unroll=2)


def carry_kernel(which, pieces, final, x_ref, *refs):
    locals_, (query, carried, rates, residues), rest = refs[:pieces], refs[pieces:pieces + 4], refs[pieces + 4:]
    if final:
        gated, squares, decay, decay8, weights, turn, sums = rest
        sums[...] = jnp.zeros_like(sums)
    else:
        gated, decay, decay8, weights, turn = rest
    count, width = query.shape
    half = carried.shape[0]
    mine = x_ref[0] if which == 0 else 1 - x_ref[0]
    rows = pl.ds(pl.multiple_of(mine * half, half), half)
    rate = rates[rows, :]
    step = jnp.exp(-rate)
    decay[...] = step
    decay8[...] = jnp.exp(-ROWS * rate)
    weights[...] = residues[rows, :] * jnp.sqrt(1.0 - step * step) * carried[...]
    groups = width // LANES // pieces

    for piece, local in enumerate(locals_):
        def group_step(group, unused):
            here = lanes(group)
            at = lanes(piece * groups + group)
            slot = turn.at[group % 2]
            gates = query[:, at].astype(F32)
            term, factor = weights[:, at], decay[:, at]
            for token in range(ROWS):
                term = term * factor
                slot[pl.ds(token, half, stride=ROWS), :] = term
            terms = [slot[m * ROWS:(m + 1) * ROWS, :] for m in range(half)]
            factors = [spread_row(decay8, m, at) for m in range(half)]
            for i in range(0, count, ROWS):
                result = local[i:i + ROWS, here] + gates[i:i + ROWS] * added(terms)
                gated[i:i + ROWS, at] = result
                if final:
                    sums[i:i + ROWS, :] += result * result
                if i + ROWS < count:
                    terms = [t * f for t, f in zip(terms, factors)]
            return unused

        lax.fori_loop(0, groups, group_step, 0)
    if final:
        squares[...] = jnp.sum(jnp.transpose(sums[...]), axis=0, keepdims=True)


def norm_kernel(parts, gated, gain, *rest):
    sums, (out, factors, buf, sems) = rest[:parts], rest[parts:]
    count, width = gated.shape
    factor = lax.rsqrt(added(part[...] for part in sums) / C + 1e-06)
    factors[...] = jnp.transpose(jnp.broadcast_to(factor, (LANES, count)))
    size = 2 * ROWS

    def copy(i):
        rows = pl.ds(pl.multiple_of(i * size, size), size)
        return pltpu.make_async_copy(buf.at[rows, :], out.at[rows, :], sems.at[i])

    def chunk_step(i, unused):
        rows = pl.ds(pl.multiple_of(i * size, size), size)
        factor = factors[rows, :]
        for group in range(width // LANES):
            at = slice(group * LANES, (group + 1) * LANES)
            buf[rows, at] = (gated[rows, at] * factor * gain[:, at]).astype(buf.dtype)
        copy(i).start()
        return unused

    lax.fori_loop(0, count // size, chunk_step, 0)
    for i in range(count // size):
        copy(i).wait()


def call(kernel, inputs, specs, outputs, out_specs=None, scratch=(), flops=0, name=None):
    size = sum(x.size * x.dtype.itemsize for x in (*inputs, *outputs))
    return pl.pallas_call(
        kernel,
        out_shape=outputs,
        in_specs=specs,
        out_specs=out_specs or [VMEM] * len(outputs),
        scratch_shapes=scratch,
        cost_estimate=pl.CostEstimate(flops=flops, bytes_accessed=size, transcendentals=0),
        compiler_params=pltpu.CompilerParams(vmem_limit_bytes=32 * 1024 * 1024),
        name=name,
    )(*inputs)


def body(ctx, tp, query, keys, values, rates, residues, skip, gain):
    count, width = keys.shape
    modes = rates.shape[0]
    half = modes // 2
    outer = ctx // 2
    f32 = lambda *shape: jax.ShapeDtypeStruct(shape, F32)
    vmem = lambda *shape: pltpu.VMEM(shape, F32)
    in_hbm = lambda x: pltpu.with_memory_space_constraint(x, pltpu.HBM)
    tied = lax.optimization_barrier
    own = lax.axis_index("ctx").astype(jnp.int32)
    z, x = own // 2, own % 2
    x_ref = x.reshape(1)
    work = 2 * half * count * width
    pair = [(i, i ^ 1) for i in range(ctx)]

    chunks = width // 256
    other, driven = call(
        lambda *refs: first_ends_kernel(chunks, *refs),
        (x_ref, in_hbm(keys), in_hbm(values), in_hbm(rates)),
        [SMEM, HBM, HBM, HBM],
        (f32(half, width), f32(count, width)),
        scratch=[
            pltpu.VMEM((count, width), keys.dtype),
            pltpu.VMEM((count, width), values.dtype),
            *[vmem(half, width)] * 4,
            vmem(2, half * ROWS, LANES),
            pltpu.SemaphoreType.DMA((2 * chunks + 1,)),
        ],
        flops=work,
        name="first_ends",
    )
    partner = lax.ppermute(other, "ctx", pair)
    (mine,) = call(
        second_ends_kernel,
        (x_ref, driven, rates),
        [SMEM, VMEM, VMEM],
        (f32(half, width),),
        scratch=[*[vmem(half, width)] * 3, vmem(2, half * ROWS, LANES)],
        flops=work,
        name="second_ends",
    )

    pieces = width // LANES // ROWS

    def local_part(part, driven):
        (local,) = call(
            lambda *refs: local_kernel(part, *refs),
            (query, driven, rates, residues, skip[None]),
            [VMEM] * 5,
            (f32(count, width // pieces),),
            scratch=[vmem(count * ROWS, LANES), vmem(modes * ROWS, LANES), vmem(modes * ROWS, LANES)],
            flops=4 * work // pieces,
            name="local_filter",
        )
        return local

    early = [local_part(part, driven) for part in range(pieces // 2)]
    partner, mine, early = tied((partner, mine, early))

    def shifted(array, by):
        return lax.ppermute(array, "ctx", [(i, (i + 2 * by) % ctx) for i in range(ctx)])

    my_rates = jnp.where(x == 0, rates[:half], rates[half:])
    step = jnp.exp(-my_rates * count)
    pair_state = jnp.where(x == 0, mine * step + partner, partner * step + mine)
    pair_state, driven = tied((pair_state, driven))

    span = min(3, outer - 1)
    moved = [shifted(pair_state, by) for by in range(span, 0, -1)]
    late = [local_part(part, driven) for part in range(pieces // 2, pieces)]
    moved, late = tied((moved, late))
    before = jnp.zeros_like(mine)
    for by, states in zip(range(span, 0, -1), moved):
        weight = jnp.exp(-my_rates * (2 * count * (by - 1)))
        before = before + jnp.where(z >= by, weight * states, 0.0)
    while span < outer - 1:
        moved = [(by, shifted(before, by)) for by in range(3 * span, 0, -span) if by < outer]
        for by, states in moved:
            weight = jnp.exp(-my_rates * (2 * count * by))
            before = before + jnp.where(z >= by, weight * states, 0.0)
        span = 4 * span

    second = before * step + jnp.where(x == 0, mine, partner)
    kept = jnp.where(x == 0, before, second)
    received = lax.ppermute(jnp.where(x == 0, second, before), "ctx", pair)

    carry_scratch = [*[vmem(half, width)] * 3, vmem(2, half * ROWS, LANES)]
    locals_ = early + late
    (halfway,) = call(
        lambda *refs: carry_kernel(0, pieces, False, *refs),
        (x_ref, *locals_, query, kept, rates, residues),
        [SMEM] + [VMEM] * (pieces + 4),
        (f32(count, width),),
        scratch=carry_scratch,
        flops=work,
        name="add_kept",
    )
    gated, squares = call(
        lambda *refs: carry_kernel(1, 1, True, *refs),
        (x_ref, halfway, query, received, rates, residues),
        [SMEM] + [VMEM] * 5,
        (f32(count, width), f32(1, count)),
        scratch=[*carry_scratch, vmem(count, LANES)],
        flops=work,
        name="add_received",
    )

    parts = [squares]
    if tp & (tp - 1) == 0:
        mask = 1
        while mask < tp:
            parts = [added(parts)]
            parts.append(lax.ppermute(parts[0], "tp", [(i, i ^ mask) for i in range(tp)]))
            mask = 2 * mask + 1
    else:
        total = squares
        for by in range(1, tp):
            total = total + lax.ppermute(squares, "tp", [(i, (i + by) % tp) for i in range(tp)])
        parts = [total]
    (out,) = call(
        lambda *refs: norm_kernel(len(parts), *refs),
        (gated, gain[None], *parts),
        [VMEM] * (2 + len(parts)),
        (jax.ShapeDtypeStruct((count, width), query.dtype),),
        out_specs=[HBM],
        scratch=[
            vmem(count, LANES),
            pltpu.VMEM((count, width), query.dtype),
            pltpu.SemaphoreType.DMA((count // (2 * ROWS),)),
        ],
        flops=2 * count * width,
        name="norm",
    )
    return out


def solution(mesh):
    ctx, tp = mesh.shape["ctx"], mesh.shape["tp"]
    in_specs = (
        P("ctx", "tp"),
        P("ctx", "tp"),
        P("ctx", "tp"),
        P(None, "tp"),
        P(None, "tp"),
        P("tp"),
        P("tp"),
    )
    return jax.shard_map(
        lambda *arrays: body(ctx, tp, *arrays),
        mesh=mesh,
        in_specs=in_specs,
        out_specs=P("ctx", "tp"),
        check_vma=False,
    )
```

```python
import jax
import jax.numpy as jnp
from jax import lax
from jax.experimental import pallas as pl
from jax.experimental.pallas import tpu as pltpu
from jax.sharding import PartitionSpec as P

C = 8192
LANES = 128
ROWS = 8
F32 = jnp.float32
VMEM = pl.BlockSpec(memory_space=pltpu.VMEM)
SMEM = pl.BlockSpec(memory_space=pltpu.SMEM)
HBM = pl.BlockSpec(memory_space=pltpu.HBM)


def lanes(group):
    return pl.ds(pl.multiple_of(group * LANES, LANES), LANES)


def added(terms):
    terms = list(terms)
    while len(terms) > 1:
        terms = [a + b for a, b in zip(terms[::2], terms[1::2])]
    return terms[0]


def spread_row(ref, row, at):
    return jnp.broadcast_to(ref[row:row + 1, at], (ROWS, LANES))


def end_states(blocks, decay, decay8, decay16, turn, out, at):
    modes = decay.shape[0]
    for mode in range(modes):
        factor = spread_row(decay16, mode, at)
        even, odd = blocks[0], blocks[1]
        for i in range(2, len(blocks), 2):
            even = even * factor + blocks[i]
            odd = odd * factor + blocks[i + 1]
        turn[mode * ROWS:(mode + 1) * ROWS, :] = even * spread_row(decay8, mode, at) + odd
    step = decay[:, at]
    state = turn[pl.ds(0, modes, stride=ROWS), :]
    for token in range(1, ROWS):
        state = state * step + turn[pl.ds(token, modes, stride=ROWS), :]
    out[:, at] = state


def set_decays(rate, decay, decay8, decay16):
    decay[...] = jnp.exp(-rate)
    decay8[...] = jnp.exp(-ROWS * rate)
    decay16[...] = jnp.exp(-2 * ROWS * rate)


def first_ends_kernel(chunks, x_ref, keys, values, rates, other, driven, key_buf, value_buf, rate_buf,
                      decay, decay8, decay16, turn, sems):
    count, width = key_buf.shape
    half = rate_buf.shape[0]
    size = width // chunks
    start = pl.multiple_of((1 - x_ref[0]) * half, half)
    rate_copy = pltpu.make_async_copy(rates.at[pl.ds(start, half), :], rate_buf, sems.at[2 * chunks])
    rate_copy.start()
    copies = []
    for i in range(chunks):
        at = pl.ds(i * size, size)
        for j, (source, target) in enumerate(((keys, key_buf), (values, value_buf))):
            copies.append(pltpu.make_async_copy(source.at[:, at], target.at[:, at], sems.at[2 * i + j]))
            copies[-1].start()
    rate_copy.wait()
    set_decays(rate_buf[...], decay, decay8, decay16)

    def group_step(group, unused):
        at = lanes(group)
        product = key_buf[:, at].astype(F32) * value_buf[:, at].astype(F32)
        driven[:, at] = product
        blocks = [product[i:i + ROWS] for i in range(0, count, ROWS)]
        end_states(blocks, decay, decay8, decay16, turn.at[group % 2], other, at)
        return unused

    groups = size // LANES
    for i in range(chunks):
        copies[2 * i].wait()
        copies[2 * i + 1].wait()
        lax.fori_loop(i * groups, (i + 1) * groups, group_step, 0, unroll=groups)


def second_ends_kernel(x_ref, driven, rates, mine, decay, decay8, decay16, turn):
    count, width = driven.shape
    half = rates.shape[0] // 2
    set_decays(rates[pl.ds(pl.multiple_of(x_ref[0] * half, half), half), :], decay, decay8, decay16)

    def group_step(group, unused):
        at = lanes(group)
        blocks = [driven[i:i + ROWS, at] for i in range(0, count, ROWS)]
        end_states(blocks, decay, decay8, decay16, turn.at[group % 2], mine, at)
        return unused

    lax.fori_loop(0, width // LANES, group_step, 0, unroll=2)


def local_kernel(part, query, driven, rates, residues, skip, out, series, decays, scales):
    count = driven.shape[0]
    modes = rates.shape[0]

    def spread(i, unused):
        here = lanes(i)
        at = lanes(part * ROWS + i)
        for mode in range(0, modes, ROWS):
            rows = pl.ds(mode * ROWS + i, ROWS, stride=ROWS)
            decay = jnp.exp(-rates[mode:mode + ROWS, at])
            decays[rows, :] = decay
            scales[rows, :] = residues[mode:mode + ROWS, at] * jnp.sqrt(1.0 - decay * decay)
        for token in range(0, count, ROWS):
            series[pl.ds(token * ROWS + i, ROWS, stride=ROWS), :] = driven[token:token + ROWS, at]
        return unused

    lax.fori_loop(0, ROWS, spread, 0, unroll=2)
    decay = [decays[m * ROWS:(m + 1) * ROWS, :] for m in range(modes)]
    scale = [scales[m * ROWS:(m + 1) * ROWS, :] for m in range(modes)]

    def token_step(token, states):
        rows = pl.ds(pl.multiple_of(token * ROWS, ROWS), ROWS)
        now = series[rows, :]
        states = [s * d + now for s, d in zip(states, decay)]
        series[rows, :] = added(s * w for s, w in zip(states, scale))
        return states

    lax.fori_loop(0, count, token_step, [jnp.zeros((ROWS, LANES), F32)] * modes, unroll=8)

    def gate(i, unused):
        here = lanes(i)
        at = lanes(part * ROWS + i)
        gates = query[:, at].astype(F32)
        for token in range(0, count, ROWS):
            filtered = series[pl.ds(token * ROWS + i, ROWS, stride=ROWS), :]
            out[token:token + ROWS, here] = gates[token:token + ROWS] * (
                filtered + skip[:, at] * driven[token:token + ROWS, at]
            )
        return unused

    lax.fori_loop(0, ROWS, gate, 0, unroll=2)


def carry_kernel(which, pieces, final, x_ref, *refs):
    locals_, (query, carried, rates, residues), rest = refs[:pieces], refs[pieces:pieces + 4], refs[pieces + 4:]
    if final:
        gated, squares, decay, decay8, weights, turn, sums = rest
        sums[...] = jnp.zeros_like(sums)
    else:
        gated, decay, decay8, weights, turn = rest
    count, width = query.shape
    half = carried.shape[0]
    mine = x_ref[0] if which == 0 else 1 - x_ref[0]
    rows = pl.ds(pl.multiple_of(mine * half, half), half)
    rate = rates[rows, :]
    step = jnp.exp(-rate)
    decay[...] = step
    decay8[...] = jnp.exp(-ROWS * rate)
    weights[...] = residues[rows, :] * jnp.sqrt(1.0 - step * step) * carried[...]
    groups = width // LANES // pieces

    for piece, local in enumerate(locals_):
        def group_step(group, unused):
            here = lanes(group)
            at = lanes(piece * groups + group)
            slot = turn.at[group % 2]
            gates = query[:, at].astype(F32)
            term, factor = weights[:, at], decay[:, at]
            for token in range(ROWS):
                term = term * factor
                slot[pl.ds(token, half, stride=ROWS), :] = term
            terms = [slot[m * ROWS:(m + 1) * ROWS, :] for m in range(half)]
            factors = [spread_row(decay8, m, at) for m in range(half)]
            for i in range(0, count, ROWS):
                result = local[i:i + ROWS, here] + gates[i:i + ROWS] * added(terms)
                gated[i:i + ROWS, at] = result
                if final:
                    sums[i:i + ROWS, :] += result * result
                if i + ROWS < count:
                    terms = [t * f for t, f in zip(terms, factors)]
            return unused

        lax.fori_loop(0, groups, group_step, 0, unroll=4)
    if final:
        squares[...] = jnp.sum(jnp.transpose(sums[...]), axis=0, keepdims=True)


def norm_kernel(parts, gated, gain, *rest):
    sums, (out, factors, buf, sems) = rest[:parts], rest[parts:]
    count, width = gated.shape
    factor = lax.rsqrt(added(part[...] for part in sums) / C + 1e-06)
    factors[...] = jnp.transpose(jnp.broadcast_to(factor, (LANES, count)))
    size = 4 * ROWS

    def copy(i):
        rows = pl.ds(pl.multiple_of(i * size, size), size)
        return pltpu.make_async_copy(buf.at[rows, :], out.at[rows, :], sems.at[i])

    def chunk_step(i, unused):
        rows = pl.ds(pl.multiple_of(i * size, size), size)
        factor = factors[rows, :]
        for group in range(width // LANES):
            at = slice(group * LANES, (group + 1) * LANES)
            buf[rows, at] = (gated[rows, at] * factor * gain[:, at]).astype(buf.dtype)
        copy(i).start()
        return unused

    lax.fori_loop(0, count // size, chunk_step, 0, unroll=count // size)
    for i in range(count // size):
        copy(i).wait()


def call(kernel, inputs, specs, outputs, out_specs=None, scratch=(), flops=0, name=None):
    size = sum(x.size * x.dtype.itemsize for x in (*inputs, *outputs))
    return pl.pallas_call(
        kernel,
        out_shape=outputs,
        in_specs=specs,
        out_specs=out_specs or [VMEM] * len(outputs),
        scratch_shapes=scratch,
        cost_estimate=pl.CostEstimate(flops=flops, bytes_accessed=size, transcendentals=0),
        compiler_params=pltpu.CompilerParams(vmem_limit_bytes=32 * 1024 * 1024),
        name=name,
    )(*inputs)


def body(ctx, tp, query, keys, values, rates, residues, skip, gain):
    count, width = keys.shape
    modes = rates.shape[0]
    half = modes // 2
    outer = ctx // 2
    f32 = lambda *shape: jax.ShapeDtypeStruct(shape, F32)
    vmem = lambda *shape: pltpu.VMEM(shape, F32)
    in_hbm = lambda x: pltpu.with_memory_space_constraint(x, pltpu.HBM)
    tied = lax.optimization_barrier
    own = lax.axis_index("ctx").astype(jnp.int32)
    z, x = own // 2, own % 2
    x_ref = x.reshape(1)
    work = 2 * half * count * width
    pair = [(i, i ^ 1) for i in range(ctx)]

    chunks = 4
    other, driven = call(
        lambda *refs: first_ends_kernel(chunks, *refs),
        (x_ref, in_hbm(keys), in_hbm(values), in_hbm(rates)),
        [SMEM, HBM, HBM, HBM],
        (f32(half, width), f32(count, width)),
        scratch=[
            pltpu.VMEM((count, width), keys.dtype),
            pltpu.VMEM((count, width), values.dtype),
            *[vmem(half, width)] * 4,
            vmem(2, half * ROWS, LANES),
            pltpu.SemaphoreType.DMA((2 * chunks + 1,)),
        ],
        flops=work,
        name="first_ends",
    )
    partner = lax.ppermute(other, "ctx", pair)
    (mine,) = call(
        second_ends_kernel,
        (x_ref, driven, rates),
        [SMEM, VMEM, VMEM],
        (f32(half, width),),
        scratch=[*[vmem(half, width)] * 3, vmem(2, half * ROWS, LANES)],
        flops=work,
        name="second_ends",
    )

    pieces = width // LANES // ROWS

    def local_part(part, driven):
        (local,) = call(
            lambda *refs: local_kernel(part, *refs),
            (query, driven, rates, residues, skip[None]),
            [VMEM] * 5,
            (f32(count, width // pieces),),
            scratch=[vmem(count * ROWS, LANES), vmem(modes * ROWS, LANES), vmem(modes * ROWS, LANES)],
            flops=4 * work // pieces,
            name="local_filter",
        )
        return local

    early = [local_part(part, driven) for part in range(pieces // 2)]
    partner, mine, early = tied((partner, mine, early))

    def shifted(array, by):
        return lax.ppermute(array, "ctx", [(i, (i + 2 * by) % ctx) for i in range(ctx)])

    my_rates = jnp.where(x == 0, rates[:half], rates[half:])
    step = jnp.exp(-my_rates * count)
    pair_state = jnp.where(x == 0, mine * step + partner, partner * step + mine)
    pair_state, driven = tied((pair_state, driven))

    span = min(3, outer - 1)
    moved = [shifted(pair_state, by) for by in range(span, 0, -1)]
    late = [local_part(part, driven) for part in range(pieces // 2, pieces)]
    moved, late = tied((moved, late))
    before = jnp.zeros_like(mine)
    for by, states in zip(range(span, 0, -1), moved):
        weight = jnp.exp(-my_rates * (2 * count * (by - 1)))
        before = before + jnp.where(z >= by, weight * states, 0.0)
    while span < outer - 1:
        moved = [(by, shifted(before, by)) for by in range(3 * span, 0, -span) if by < outer]
        for by, states in moved:
            weight = jnp.exp(-my_rates * (2 * count * by))
            before = before + jnp.where(z >= by, weight * states, 0.0)
        span = 4 * span

    second = before * step + jnp.where(x == 0, mine, partner)
    kept = jnp.where(x == 0, before, second)
    received = lax.ppermute(jnp.where(x == 0, second, before), "ctx", pair)

    carry_scratch = [*[vmem(half, width)] * 3, vmem(2, half * ROWS, LANES)]
    locals_ = early + late
    (halfway,) = call(
        lambda *refs: carry_kernel(0, pieces, False, *refs),
        (x_ref, *locals_, query, kept, rates, residues),
        [SMEM] + [VMEM] * (pieces + 4),
        (f32(count, width),),
        scratch=carry_scratch,
        flops=work,
        name="add_kept",
    )
    gated, squares = call(
        lambda *refs: carry_kernel(1, 1, True, *refs),
        (x_ref, halfway, query, received, rates, residues),
        [SMEM] + [VMEM] * 5,
        (f32(count, width), f32(1, count)),
        scratch=[*carry_scratch, vmem(count, LANES)],
        flops=work,
        name="add_received",
    )

    parts = [squares] + [
        lax.ppermute(squares, "tp", [(i, i ^ by) for i in range(tp)]) for by in (1, 2, 3)
    ]
    (out,) = call(
        lambda *refs: norm_kernel(len(parts), *refs),
        (gated, gain[None], *parts),
        [VMEM] * (2 + len(parts)),
        (jax.ShapeDtypeStruct((count, width), query.dtype),),
        out_specs=[HBM],
        scratch=[
            vmem(count, LANES),
            pltpu.VMEM((count, width), query.dtype),
            pltpu.SemaphoreType.DMA((count // (4 * ROWS),)),
        ],
        flops=2 * count * width,
        name="norm",
    )
    return out


def solution(mesh):
    ctx, tp = mesh.shape["ctx"], mesh.shape["tp"]
    in_specs = (
        P("ctx", "tp"),
        P("ctx", "tp"),
        P("ctx", "tp"),
        P(None, "tp"),
        P(None, "tp"),
        P("tp"),
        P("tp"),
    )
    return jax.shard_map(
        lambda *arrays: body(ctx, tp, *arrays),
        mesh=mesh,
        in_specs=in_specs,
        out_specs=P("ctx", "tp"),
        check_vma=False,
    )
```

```python
import jax
import jax.numpy as jnp
from jax import lax
from jax.experimental import pallas as pl
from jax.experimental.pallas import tpu as pltpu
from jax.sharding import PartitionSpec as P

C = 8192
LANES = 128
ROWS = 8
F32 = jnp.float32
VMEM = pl.BlockSpec(memory_space=pltpu.VMEM)
SMEM = pl.BlockSpec(memory_space=pltpu.SMEM)
HBM = pl.BlockSpec(memory_space=pltpu.HBM)


def lanes(group):
    return pl.ds(pl.multiple_of(group * LANES, LANES), LANES)


def added(terms):
    terms = list(terms)
    while len(terms) > 1:
        terms = [a + b for a, b in zip(terms[::2], terms[1::2])]
    return terms[0]


def spread_row(ref, row, at):
    return jnp.broadcast_to(ref[row:row + 1, at], (ROWS, LANES))


def end_states(blocks, decay, decay8, decay16, turn, out, at):
    modes = decay.shape[0]
    for mode in range(modes):
        factor = spread_row(decay16, mode, at)
        even, odd = blocks[0], blocks[1]
        for i in range(2, len(blocks), 2):
            even = even * factor + blocks[i]
            odd = odd * factor + blocks[i + 1]
        turn[mode * ROWS:(mode + 1) * ROWS, :] = even * spread_row(decay8, mode, at) + odd
    step = decay[:, at]
    state = turn[pl.ds(0, modes, stride=ROWS), :]
    for token in range(1, ROWS):
        state = state * step + turn[pl.ds(token, modes, stride=ROWS), :]
    out[:, at] = state


def set_decays(rate, decay, decay8, decay16):
    decay[...] = jnp.exp(-rate)
    decay8[...] = jnp.exp(-ROWS * rate)
    decay16[...] = jnp.exp(-2 * ROWS * rate)


def first_ends_kernel(chunks, x_ref, keys, values, rates, other, driven, key_buf, value_buf, rate_buf,
                      decay, decay8, decay16, turn, sems):
    count, width = key_buf.shape
    half = rate_buf.shape[0]
    size = width // chunks
    start = pl.multiple_of((1 - x_ref[0]) * half, half)
    rate_copy = pltpu.make_async_copy(rates.at[pl.ds(start, half), :], rate_buf, sems.at[2 * chunks])
    rate_copy.start()
    copies = []
    for i in range(chunks):
        at = pl.ds(i * size, size)
        for j, (source, target) in enumerate(((keys, key_buf), (values, value_buf))):
            copies.append(pltpu.make_async_copy(source.at[:, at], target.at[:, at], sems.at[2 * i + j]))
            copies[-1].start()
    rate_copy.wait()
    set_decays(rate_buf[...], decay, decay8, decay16)

    def group_step(group, unused):
        at = lanes(group)
        product = key_buf[:, at].astype(F32) * value_buf[:, at].astype(F32)
        driven[:, at] = product
        blocks = [product[i:i + ROWS] for i in range(0, count, ROWS)]
        end_states(blocks, decay, decay8, decay16, turn.at[group % 2], other, at)
        return unused

    groups = size // LANES
    for i in range(chunks):
        copies[2 * i].wait()
        copies[2 * i + 1].wait()
        lax.fori_loop(i * groups, (i + 1) * groups, group_step, 0, unroll=groups)


def second_ends_kernel(x_ref, driven, rates, mine, decay, decay8, decay16, turn):
    count, width = driven.shape
    half = rates.shape[0] // 2
    set_decays(rates[pl.ds(pl.multiple_of(x_ref[0] * half, half), half), :], decay, decay8, decay16)

    def group_step(group, unused):
        at = lanes(group)
        blocks = [driven[i:i + ROWS, at] for i in range(0, count, ROWS)]
        end_states(blocks, decay, decay8, decay16, turn.at[group % 2], mine, at)
        return unused

    lax.fori_loop(0, width // LANES, group_step, 0, unroll=2)


def local_kernel(part, query, driven, rates, residues, skip, out, series, decays, scales):
    count = driven.shape[0]
    modes = rates.shape[0]

    def spread(i, unused):
        here = lanes(i)
        at = lanes(part * ROWS + i)
        for mode in range(0, modes, ROWS):
            rows = pl.ds(mode * ROWS + i, ROWS, stride=ROWS)
            decay = jnp.exp(-rates[mode:mode + ROWS, at])
            decays[rows, :] = decay
            scales[rows, :] = residues[mode:mode + ROWS, at] * jnp.sqrt(1.0 - decay * decay)
        for token in range(0, count, ROWS):
            series[pl.ds(token * ROWS + i, ROWS, stride=ROWS), :] = driven[token:token + ROWS, at]
        return unused

    lax.fori_loop(0, ROWS, spread, 0, unroll=2)
    decay = [decays[m * ROWS:(m + 1) * ROWS, :] for m in range(modes)]
    scale = [scales[m * ROWS:(m + 1) * ROWS, :] for m in range(modes)]

    def token_step(token, states):
        rows = pl.ds(pl.multiple_of(token * ROWS, ROWS), ROWS)
        now = series[rows, :]
        states = [s * d + now for s, d in zip(states, decay)]
        series[rows, :] = added(s * w for s, w in zip(states, scale))
        return states

    lax.fori_loop(0, count, token_step, [jnp.zeros((ROWS, LANES), F32)] * modes, unroll=8)

    def gate(i, unused):
        here = lanes(i)
        at = lanes(part * ROWS + i)
        gates = query[:, at].astype(F32)
        for token in range(0, count, ROWS):
            filtered = series[pl.ds(token * ROWS + i, ROWS, stride=ROWS), :]
            out[token:token + ROWS, here] = gates[token:token + ROWS] * (
                filtered + skip[:, at] * driven[token:token + ROWS, at]
            )
        return unused

    lax.fori_loop(0, ROWS, gate, 0, unroll=2)


def carry_kernel(which, pieces, final, x_ref, *refs):
    locals_, (query, carried, rates, residues), rest = refs[:pieces], refs[pieces:pieces + 4], refs[pieces + 4:]
    if final:
        gated, squares, decay, decay8, weights, turn, sums = rest
        sums[...] = jnp.zeros_like(sums)
    else:
        gated, decay, decay8, weights, turn = rest
    count, width = query.shape
    half = carried.shape[0]
    mine = x_ref[0] if which == 0 else 1 - x_ref[0]
    rows = pl.ds(pl.multiple_of(mine * half, half), half)
    rate = rates[rows, :]
    step = jnp.exp(-rate)
    decay[...] = step
    decay8[...] = jnp.exp(-ROWS * rate)
    weights[...] = residues[rows, :] * jnp.sqrt(1.0 - step * step) * carried[...]
    groups = width // LANES // pieces

    for piece, local in enumerate(locals_):
        def group_step(group, unused):
            here = lanes(group)
            at = lanes(piece * groups + group)
            slot = turn.at[group % 2]
            gates = query[:, at].astype(F32)
            term, factor = weights[:, at], decay[:, at]
            for token in range(ROWS):
                term = term * factor
                slot[pl.ds(token, half, stride=ROWS), :] = term
            terms = [slot[m * ROWS:(m + 1) * ROWS, :] for m in range(half)]
            factors = [spread_row(decay8, m, at) for m in range(half)]
            for i in range(0, count, ROWS):
                result = local[i:i + ROWS, here] + gates[i:i + ROWS] * added(terms)
                gated[i:i + ROWS, at] = result
                if final:
                    sums[i:i + ROWS, :] += result * result
                if i + ROWS < count:
                    terms = [t * f for t, f in zip(terms, factors)]
            return unused

        lax.fori_loop(0, groups, group_step, 0, unroll=4)
    if final:
        squares[...] = jnp.sum(jnp.transpose(sums[...]), axis=0, keepdims=True)


def norm_kernel(parts, gated, gain, *rest):
    sums, (out, factors, buf, sems) = rest[:parts], rest[parts:]
    count, width = gated.shape
    factor = lax.rsqrt(added(part[...] for part in sums) / C + 1e-06)
    factors[...] = jnp.transpose(jnp.broadcast_to(factor, (LANES, count)))
    size = 4 * ROWS

    def copy(i):
        rows = pl.ds(pl.multiple_of(i * size, size), size)
        return pltpu.make_async_copy(buf.at[rows, :], out.at[rows, :], sems.at[i])

    def chunk_step(i, unused):
        rows = pl.ds(pl.multiple_of(i * size, size), size)
        factor = factors[rows, :]
        for group in range(width // LANES):
            at = slice(group * LANES, (group + 1) * LANES)
            buf[rows, at] = (gated[rows, at] * factor * gain[:, at]).astype(buf.dtype)
        copy(i).start()
        return unused

    lax.fori_loop(0, count // size, chunk_step, 0, unroll=count // size)
    for i in range(count // size):
        copy(i).wait()


def call(kernel, inputs, specs, outputs, out_specs=None, scratch=(), flops=0, name=None):
    size = sum(x.size * x.dtype.itemsize for x in (*inputs, *outputs))
    return pl.pallas_call(
        kernel,
        out_shape=outputs,
        in_specs=specs,
        out_specs=out_specs or [VMEM] * len(outputs),
        scratch_shapes=scratch,
        cost_estimate=pl.CostEstimate(flops=flops, bytes_accessed=size, transcendentals=0),
        compiler_params=pltpu.CompilerParams(vmem_limit_bytes=32 * 1024 * 1024),
        name=name,
    )(*inputs)


def body(ctx, tp, query, keys, values, rates, residues, skip, gain):
    count, width = keys.shape
    modes = rates.shape[0]
    half = modes // 2
    outer = ctx // 2
    f32 = lambda *shape: jax.ShapeDtypeStruct(shape, F32)
    vmem = lambda *shape: pltpu.VMEM(shape, F32)
    in_hbm = lambda x: pltpu.with_memory_space_constraint(x, pltpu.HBM)
    tied = lax.optimization_barrier
    own = lax.axis_index("ctx").astype(jnp.int32)
    z, x = own // 2, own % 2
    x_ref = x.reshape(1)
    work = 2 * half * count * width
    pair = [(i, i ^ 1) for i in range(ctx)]

    chunks = 4
    other, driven = call(
        lambda *refs: first_ends_kernel(chunks, *refs),
        (x_ref, in_hbm(keys), in_hbm(values), in_hbm(rates)),
        [SMEM, HBM, HBM, HBM],
        (f32(half, width), f32(count, width)),
        scratch=[
            pltpu.VMEM((count, width), keys.dtype),
            pltpu.VMEM((count, width), values.dtype),
            *[vmem(half, width)] * 4,
            vmem(2, half * ROWS, LANES),
            pltpu.SemaphoreType.DMA((2 * chunks + 1,)),
        ],
        flops=work,
        name="first_ends",
    )
    partner = lax.ppermute(other, "ctx", pair)
    (mine,) = call(
        second_ends_kernel,
        (x_ref, driven, rates),
        [SMEM, VMEM, VMEM],
        (f32(half, width),),
        scratch=[*[vmem(half, width)] * 3, vmem(2, half * ROWS, LANES)],
        flops=work,
        name="second_ends",
    )

    pieces = width // LANES // ROWS

    def local_part(part, driven):
        (local,) = call(
            lambda *refs: local_kernel(part, *refs),
            (query, driven, rates, residues, skip[None]),
            [VMEM] * 5,
            (f32(count, width // pieces),),
            scratch=[vmem(count * ROWS, LANES), vmem(modes * ROWS, LANES), vmem(modes * ROWS, LANES)],
            flops=4 * work // pieces,
            name="local_filter",
        )
        return local

    early = [local_part(part, driven) for part in range(pieces // 2)]
    partner, mine, early = tied((partner, mine, early))

    def shifted(array, by):
        return lax.ppermute(array, "ctx", [(i, (i + 2 * by) % ctx) for i in range(ctx)])

    my_rates = jnp.where(x == 0, rates[:half], rates[half:])
    step = jnp.exp(-my_rates * count)
    pair_state = jnp.where(x == 0, mine * step + partner, partner * step + mine)
    pair_state, driven = tied((pair_state, driven))

    def late_parts():
        return [local_part(part, driven) for part in range(pieces // 2, pieces)]

    if outer == 4 and tp % 2 == 0:
        def moved(array, targets):
            def target(i, j):
                to = targets[i // 2]
                return (2 * to + i % 2) * tp + (j if to != i // 2 else j ^ 1)

            links = [(i * tp + j, target(i, j)) for i in range(ctx) for j in range(tp)]
            return lax.ppermute(array, ("ctx", "tp"), links)

        span = jnp.exp(-my_rates * (2 * count))
        first_move = moved(pair_state, (1, 2, 0, 3))
        second_move = moved(pair_state, (0, 1, 3, 2))
        third_move = moved(pair_state, (2, 1, 0, 3))
        late = late_parts()
        first_move, late = tied((first_move, late))
        both = jnp.where(z == 1, span * first_move + pair_state, pair_state)
        handed = moved(both, (0, 3, 1, 2))
        before = jnp.where(
            z == 0,
            0.0,
            jnp.where(z == 1, first_move, jnp.where(z == 2, first_move + span * third_move, second_move + span * handed)),
        )
    else:
        span = min(3, outer - 1)
        parts = [shifted(pair_state, by) for by in range(span, 0, -1)]
        late = late_parts()
        parts, late = tied((parts, late))
        before = jnp.zeros_like(mine)
        for by, states in zip(range(span, 0, -1), parts):
            weight = jnp.exp(-my_rates * (2 * count * (by - 1)))
            before = before + jnp.where(z >= by, weight * states, 0.0)
        while span < outer - 1:
            parts = [(by, shifted(before, by)) for by in range(3 * span, 0, -span) if by < outer]
            for by, states in parts:
                weight = jnp.exp(-my_rates * (2 * count * by))
                before = before + jnp.where(z >= by, weight * states, 0.0)
            span = 4 * span

    second = before * step + jnp.where(x == 0, mine, partner)
    kept = jnp.where(x == 0, before, second)
    received = lax.ppermute(jnp.where(x == 0, second, before), "ctx", pair)

    carry_scratch = [*[vmem(half, width)] * 3, vmem(2, half * ROWS, LANES)]
    locals_ = early + late
    (halfway,) = call(
        lambda *refs: carry_kernel(0, pieces, False, *refs),
        (x_ref, *locals_, query, kept, rates, residues),
        [SMEM] + [VMEM] * (pieces + 4),
        (f32(count, width),),
        scratch=carry_scratch,
        flops=work,
        name="add_kept",
    )
    gated, squares = call(
        lambda *refs: carry_kernel(1, 1, True, *refs),
        (x_ref, halfway, query, received, rates, residues),
        [SMEM] + [VMEM] * 5,
        (f32(count, width), f32(1, count)),
        scratch=[*carry_scratch, vmem(count, LANES)],
        flops=work,
        name="add_received",
    )

    parts = [squares] + [
        lax.ppermute(squares, "tp", [(i, i ^ by) for i in range(tp)]) for by in (1, 2, 3)
    ]
    (out,) = call(
        lambda *refs: norm_kernel(len(parts), *refs),
        (gated, gain[None], *parts),
        [VMEM] * (2 + len(parts)),
        (jax.ShapeDtypeStruct((count, width), query.dtype),),
        out_specs=[HBM],
        scratch=[
            vmem(count, LANES),
            pltpu.VMEM((count, width), query.dtype),
            pltpu.SemaphoreType.DMA((count // (4 * ROWS),)),
        ],
        flops=2 * count * width,
        name="norm",
    )
    return out


def solution(mesh):
    ctx, tp = mesh.shape["ctx"], mesh.shape["tp"]
    in_specs = (
        P("ctx", "tp"),
        P("ctx", "tp"),
        P("ctx", "tp"),
        P(None, "tp"),
        P(None, "tp"),
        P("tp"),
        P("tp"),
    )
    return jax.shard_map(
        lambda *arrays: body(ctx, tp, *arrays),
        mesh=mesh,
        in_specs=in_specs,
        out_specs=P("ctx", "tp"),
        check_vma=False,
    )
```

```python
import jax
import jax.numpy as jnp
from jax import lax
from jax.experimental import pallas as pl
from jax.experimental.pallas import tpu as pltpu
from jax.sharding import PartitionSpec as P

C = 8192
LANES = 128
ROWS = 8
F32 = jnp.float32
VMEM = pl.BlockSpec(memory_space=pltpu.VMEM)
SMEM = pl.BlockSpec(memory_space=pltpu.SMEM)
HBM = pl.BlockSpec(memory_space=pltpu.HBM)


def lanes(group):
    return pl.ds(pl.multiple_of(group * LANES, LANES), LANES)


def added(terms):
    terms = list(terms)
    while len(terms) > 1:
        odd = terms[len(terms) - len(terms) % 2:]
        terms = [a + b for a, b in zip(terms[::2], terms[1::2])] + odd
    return terms[0]


def spread_row(ref, row, at):
    return jnp.broadcast_to(ref[row:row + 1, at], (ROWS, LANES))


def end_states(blocks, decay, decay8, decay16, turn, out, at):
    modes = decay.shape[0]
    for mode in range(modes):
        factor = spread_row(decay16, mode, at)
        even, odd = blocks[0], blocks[1]
        for i in range(2, len(blocks), 2):
            even = even * factor + blocks[i]
            odd = odd * factor + blocks[i + 1]
        turn[mode * ROWS:(mode + 1) * ROWS, :] = even * spread_row(decay8, mode, at) + odd
    step = decay[:, at]
    state = turn[pl.ds(0, modes, stride=ROWS), :]
    for token in range(1, ROWS):
        state = state * step + turn[pl.ds(token, modes, stride=ROWS), :]
    out[:, at] = state


def set_decays(rate, decay, decay8, decay16):
    decay[...] = jnp.exp(-rate)
    decay8[...] = jnp.exp(-ROWS * rate)
    decay16[...] = jnp.exp(-2 * ROWS * rate)


def first_ends_kernel(chunks, x_ref, keys, values, rates, other, driven, key_buf, value_buf, rate_buf,
                      decay, decay8, decay16, turn, sems):
    count, width = key_buf.shape
    half = rate_buf.shape[0]
    size = width // chunks
    start = pl.multiple_of((1 - x_ref[0]) * half, half)
    rate_copy = pltpu.make_async_copy(rates.at[pl.ds(start, half), :], rate_buf, sems.at[2 * chunks])
    rate_copy.start()
    copies = []
    for i in range(chunks):
        at = pl.ds(i * size, size)
        for j, (source, target) in enumerate(((keys, key_buf), (values, value_buf))):
            copies.append(pltpu.make_async_copy(source.at[:, at], target.at[:, at], sems.at[2 * i + j]))
            copies[-1].start()
    rate_copy.wait()
    set_decays(rate_buf[...], decay, decay8, decay16)

    def group_step(group, unused):
        at = lanes(group)
        product = key_buf[:, at].astype(F32) * value_buf[:, at].astype(F32)
        driven[:, at] = product
        blocks = [product[i:i + ROWS] for i in range(0, count, ROWS)]
        end_states(blocks, decay, decay8, decay16, turn.at[group % 2], other, at)
        return unused

    groups = size // LANES
    for i in range(chunks):
        copies[2 * i].wait()
        copies[2 * i + 1].wait()
        lax.fori_loop(i * groups, (i + 1) * groups, group_step, 0, unroll=groups)


def second_ends_kernel(x_ref, driven, rates, mine, decay, decay8, decay16, turn):
    count, width = driven.shape
    half = rates.shape[0] // 2
    set_decays(rates[pl.ds(pl.multiple_of(x_ref[0] * half, half), half), :], decay, decay8, decay16)

    def group_step(group, unused):
        at = lanes(group)
        blocks = [driven[i:i + ROWS, at] for i in range(0, count, ROWS)]
        end_states(blocks, decay, decay8, decay16, turn.at[group % 2], mine, at)
        return unused

    lax.fori_loop(0, width // LANES, group_step, 0, unroll=2)


def local_kernel(part, query, driven, rates, residues, skip, out, series, decays, scales):
    count = driven.shape[0]
    modes = rates.shape[0]

    def spread(i, unused):
        here = lanes(i)
        at = lanes(part * ROWS + i)
        for mode in range(0, modes, ROWS):
            rows = pl.ds(mode * ROWS + i, ROWS, stride=ROWS)
            decay = jnp.exp(-rates[mode:mode + ROWS, at])
            decays[rows, :] = decay
            scales[rows, :] = residues[mode:mode + ROWS, at] * jnp.sqrt(1.0 - decay * decay)
        for token in range(0, count, ROWS):
            series[pl.ds(token * ROWS + i, ROWS, stride=ROWS), :] = driven[token:token + ROWS, at]
        return unused

    lax.fori_loop(0, ROWS, spread, 0, unroll=2)
    decay = [decays[m * ROWS:(m + 1) * ROWS, :] for m in range(modes)]
    scale = [scales[m * ROWS:(m + 1) * ROWS, :] for m in range(modes)]

    def token_step(token, states):
        rows = pl.ds(pl.multiple_of(token * ROWS, ROWS), ROWS)
        now = series[rows, :]
        states = [s * d + now for s, d in zip(states, decay)]
        series[rows, :] = added(s * w for s, w in zip(states, scale))
        return states

    lax.fori_loop(0, count, token_step, [jnp.zeros((ROWS, LANES), F32)] * modes, unroll=8)

    def gate(i, unused):
        here = lanes(i)
        at = lanes(part * ROWS + i)
        gates = query[:, at].astype(F32)
        for token in range(0, count, ROWS):
            filtered = series[pl.ds(token * ROWS + i, ROWS, stride=ROWS), :]
            out[token:token + ROWS, here] = gates[token:token + ROWS] * (
                filtered + skip[:, at] * driven[token:token + ROWS, at]
            )
        return unused

    lax.fori_loop(0, ROWS, gate, 0, unroll=2)


def carry_kernel(which, pieces, final, x_ref, *refs):
    locals_, (query, carried, rates, residues), rest = refs[:pieces], refs[pieces:pieces + 4], refs[pieces + 4:]
    if final:
        gated, squares, decay, decay8, weights, turn, sums = rest
        sums[...] = jnp.zeros_like(sums)
    else:
        gated, decay, decay8, weights, turn = rest
    count, width = query.shape
    half = carried.shape[0]
    mine = x_ref[0] if which == 0 else 1 - x_ref[0]
    rows = pl.ds(pl.multiple_of(mine * half, half), half)
    rate = rates[rows, :]
    step = jnp.exp(-rate)
    decay[...] = step
    decay8[...] = jnp.exp(-ROWS * rate)
    weights[...] = residues[rows, :] * jnp.sqrt(1.0 - step * step) * carried[...]
    groups = width // LANES // pieces

    for piece, local in enumerate(locals_):
        def group_step(group, unused):
            here = lanes(group)
            at = lanes(piece * groups + group)
            slot = turn.at[group % 2]
            gates = query[:, at].astype(F32)
            term, factor = weights[:, at], decay[:, at]
            for token in range(ROWS):
                term = term * factor
                slot[pl.ds(token, half, stride=ROWS), :] = term
            terms = [slot[m * ROWS:(m + 1) * ROWS, :] for m in range(half)]
            factors = [spread_row(decay8, m, at) for m in range(half)]
            for i in range(0, count, ROWS):
                result = local[i:i + ROWS, here] + gates[i:i + ROWS] * added(terms)
                gated[i:i + ROWS, at] = result
                if final:
                    sums[i:i + ROWS, :] += result * result
                if i + ROWS < count:
                    terms = [t * f for t, f in zip(terms, factors)]
            return unused

        lax.fori_loop(0, groups, group_step, 0, unroll=4)
    if final:
        squares[...] = jnp.sum(jnp.transpose(sums[...]), axis=0, keepdims=True)


def norm_kernel(parts, gated, gain, *rest):
    sums, (out, factors, buf, sems) = rest[:parts], rest[parts:]
    count, width = gated.shape
    factor = lax.rsqrt(added(part[...] for part in sums) / C + 1e-06)
    factors[...] = jnp.transpose(jnp.broadcast_to(factor, (LANES, count)))
    size = 4 * ROWS

    def copy(i):
        rows = pl.ds(pl.multiple_of(i * size, size), size)
        return pltpu.make_async_copy(buf.at[rows, :], out.at[rows, :], sems.at[i])

    def chunk_step(i, unused):
        rows = pl.ds(pl.multiple_of(i * size, size), size)
        factor = factors[rows, :]
        for group in range(width // LANES):
            at = slice(group * LANES, (group + 1) * LANES)
            buf[rows, at] = (gated[rows, at] * factor * gain[:, at]).astype(buf.dtype)
        copy(i).start()
        return unused

    lax.fori_loop(0, count // size, chunk_step, 0, unroll=count // size)
    for i in range(count // size):
        copy(i).wait()


def call(kernel, inputs, specs, outputs, out_specs=None, scratch=(), flops=0, name=None):
    size = sum(x.size * x.dtype.itemsize for x in (*inputs, *outputs))
    return pl.pallas_call(
        kernel,
        out_shape=outputs,
        in_specs=specs,
        out_specs=out_specs or [VMEM] * len(outputs),
        scratch_shapes=scratch,
        cost_estimate=pl.CostEstimate(flops=flops, bytes_accessed=size, transcendentals=0),
        compiler_params=pltpu.CompilerParams(vmem_limit_bytes=32 * 1024 * 1024),
        name=name,
    )(*inputs)


def body(ctx, tp, query, keys, values, rates, residues, skip, gain):
    count, width = keys.shape
    modes = rates.shape[0]
    half = modes // 2
    outer = ctx // 2
    f32 = lambda *shape: jax.ShapeDtypeStruct(shape, F32)
    vmem = lambda *shape: pltpu.VMEM(shape, F32)
    in_hbm = lambda x: pltpu.with_memory_space_constraint(x, pltpu.HBM)
    tied = lax.optimization_barrier
    own = lax.axis_index("ctx").astype(jnp.int32)
    z, x = own // 2, own % 2
    x_ref = x.reshape(1)
    work = 2 * half * count * width
    pair = [(i, i ^ 1) for i in range(ctx)]

    chunks = 4
    other, driven = call(
        lambda *refs: first_ends_kernel(chunks, *refs),
        (x_ref, in_hbm(keys), in_hbm(values), in_hbm(rates)),
        [SMEM, HBM, HBM, HBM],
        (f32(half, width), f32(count, width)),
        scratch=[
            pltpu.VMEM((count, width), keys.dtype),
            pltpu.VMEM((count, width), values.dtype),
            *[vmem(half, width)] * 4,
            vmem(2, half * ROWS, LANES),
            pltpu.SemaphoreType.DMA((2 * chunks + 1,)),
        ],
        flops=work,
        name="first_ends",
    )
    partner = lax.ppermute(other, "ctx", pair)
    (mine,) = call(
        second_ends_kernel,
        (x_ref, driven, rates),
        [SMEM, VMEM, VMEM],
        (f32(half, width),),
        scratch=[*[vmem(half, width)] * 3, vmem(2, half * ROWS, LANES)],
        flops=work,
        name="second_ends",
    )

    pieces = width // LANES // ROWS

    def local_part(part, driven):
        (local,) = call(
            lambda *refs: local_kernel(part, *refs),
            (query, driven, rates, residues, skip[None]),
            [VMEM] * 5,
            (f32(count, width // pieces),),
            scratch=[vmem(count * ROWS, LANES), vmem(modes * ROWS, LANES), vmem(modes * ROWS, LANES)],
            flops=4 * work // pieces,
            name="local_filter",
        )
        return local

    early = [local_part(part, driven) for part in range(pieces // 2)]
    partner, mine, early = tied((partner, mine, early))

    def shifted(array, by):
        return lax.ppermute(array, "ctx", [(i, (i + 2 * by) % ctx) for i in range(ctx)])

    my_rates = jnp.where(x == 0, rates[:half], rates[half:])
    step = jnp.exp(-my_rates * count)
    pair_state = jnp.where(x == 0, mine * step + partner, partner * step + mine)
    pair_state, driven = tied((pair_state, driven))

    def late_parts():
        return [local_part(part, driven) for part in range(pieces // 2, pieces)]

    if outer == 4 and tp % 2 == 0:
        def moved(array, targets):
            def target(i, j):
                to = targets[i // 2]
                return (2 * to + i % 2) * tp + (j if to != i // 2 else j ^ 1)

            links = [(i * tp + j, target(i, j)) for i in range(ctx) for j in range(tp)]
            return lax.ppermute(array, ("ctx", "tp"), links)

        span = jnp.exp(-my_rates * (2 * count))
        first_move = moved(pair_state, (1, 2, 0, 3))
        second_move = moved(pair_state, (0, 1, 3, 2))
        third_move = moved(pair_state, (2, 1, 0, 3))
        late = late_parts()
        first_move, late = tied((first_move, late))
        both = jnp.where(z == 1, span * first_move + pair_state, pair_state)
        handed = moved(both, (0, 3, 1, 2))
        before = jnp.where(
            z == 0,
            0.0,
            jnp.where(z == 1, first_move, jnp.where(z == 2, first_move + span * third_move, second_move + span * handed)),
        )
    else:
        span = min(3, outer - 1)
        parts = [shifted(pair_state, by) for by in range(span, 0, -1)]
        late = late_parts()
        parts, late = tied((parts, late))
        before = jnp.zeros_like(mine)
        for by, states in zip(range(span, 0, -1), parts):
            weight = jnp.exp(-my_rates * (2 * count * (by - 1)))
            before = before + jnp.where(z >= by, weight * states, 0.0)
        while span < outer - 1:
            parts = [(by, shifted(before, by)) for by in range(3 * span, 0, -span) if by < outer]
            for by, states in parts:
                weight = jnp.exp(-my_rates * (2 * count * by))
                before = before + jnp.where(z >= by, weight * states, 0.0)
            span = 4 * span

    second = before * step + jnp.where(x == 0, mine, partner)
    kept = jnp.where(x == 0, before, second)
    received = lax.ppermute(jnp.where(x == 0, second, before), "ctx", pair)

    carry_scratch = [*[vmem(half, width)] * 3, vmem(2, half * ROWS, LANES)]
    locals_ = early + late
    (halfway,) = call(
        lambda *refs: carry_kernel(0, pieces, False, *refs),
        (x_ref, *locals_, query, kept, rates, residues),
        [SMEM] + [VMEM] * (pieces + 4),
        (f32(count, width),),
        scratch=carry_scratch,
        flops=work,
        name="add_kept",
    )
    gated, squares = call(
        lambda *refs: carry_kernel(1, 1, True, *refs),
        (x_ref, halfway, query, received, rates, residues),
        [SMEM] + [VMEM] * 5,
        (f32(count, width), f32(1, count)),
        scratch=[*carry_scratch, vmem(count, LANES)],
        flops=work,
        name="add_received",
    )

    def across(i, by):
        return i ^ by if tp & (tp - 1) == 0 else (i + by) % tp

    parts = [squares] + [
        lax.ppermute(squares, "tp", [(i, across(i, by)) for i in range(tp)]) for by in range(1, tp)
    ]
    (out,) = call(
        lambda *refs: norm_kernel(len(parts), *refs),
        (gated, gain[None], *parts),
        [VMEM] * (2 + len(parts)),
        (jax.ShapeDtypeStruct((count, width), query.dtype),),
        out_specs=[HBM],
        scratch=[
            vmem(count, LANES),
            pltpu.VMEM((count, width), query.dtype),
            pltpu.SemaphoreType.DMA((count // (4 * ROWS),)),
        ],
        flops=2 * count * width,
        name="norm",
    )
    return out


def solution(mesh):
    ctx, tp = mesh.shape["ctx"], mesh.shape["tp"]
    in_specs = (
        P("ctx", "tp"),
        P("ctx", "tp"),
        P("ctx", "tp"),
        P(None, "tp"),
        P(None, "tp"),
        P("tp"),
        P("tp"),
    )
    return jax.shard_map(
        lambda *arrays: body(ctx, tp, *arrays),
        mesh=mesh,
        in_specs=in_specs,
        out_specs=P("ctx", "tp"),
        check_vma=False,
    )
```

```python
import jax
import jax.numpy as jnp
from jax import lax
from jax.experimental import pallas as pl
from jax.experimental.pallas import tpu as pltpu
from jax.sharding import PartitionSpec as P

C = 8192
LANES = 128
ROWS = 8
F32 = jnp.float32
VMEM = pl.BlockSpec(memory_space=pltpu.VMEM)
SMEM = pl.BlockSpec(memory_space=pltpu.SMEM)
HBM = pl.BlockSpec(memory_space=pltpu.HBM)


def lanes(group):
    return pl.ds(pl.multiple_of(group * LANES, LANES), LANES)


def added(terms):
    terms = list(terms)
    while len(terms) > 1:
        odd = terms[len(terms) - len(terms) % 2:]
        terms = [a + b for a, b in zip(terms[::2], terms[1::2])] + odd
    return terms[0]


def spread_row(ref, row, at):
    return jnp.broadcast_to(ref[row:row + 1, at], (ROWS, LANES))


def end_states(blocks, decay, decay8, decay16, turn, out, at):
    modes = decay.shape[0]
    for mode in range(modes):
        factor = spread_row(decay16, mode, at)
        even, odd = blocks[0], blocks[1]
        for i in range(2, len(blocks), 2):
            even = even * factor + blocks[i]
            odd = odd * factor + blocks[i + 1]
        turn[mode * ROWS:(mode + 1) * ROWS, :] = even * spread_row(decay8, mode, at) + odd
    step = decay[:, at]
    state = turn[pl.ds(0, modes, stride=ROWS), :]
    for token in range(1, ROWS):
        state = state * step + turn[pl.ds(token, modes, stride=ROWS), :]
    out[:, at] = state


def set_decays(rate, decay, decay8, decay16):
    decay[...] = jnp.exp(-rate)
    decay8[...] = jnp.exp(-ROWS * rate)
    decay16[...] = jnp.exp(-2 * ROWS * rate)


def first_ends_kernel(chunks, x_ref, keys, values, rates, other, driven, key_buf, value_buf, rate_buf,
                      decay, decay8, decay16, turn, sems):
    count, width = key_buf.shape
    half = rate_buf.shape[0]
    size = width // chunks
    start = pl.multiple_of((1 - x_ref[0]) * half, half)
    rate_copy = pltpu.make_async_copy(rates.at[pl.ds(start, half), :], rate_buf, sems.at[2 * chunks])
    rate_copy.start()
    copies = []
    for i in range(chunks):
        at = pl.ds(i * size, size)
        for j, (source, target) in enumerate(((keys, key_buf), (values, value_buf))):
            copies.append(pltpu.make_async_copy(source.at[:, at], target.at[:, at], sems.at[2 * i + j]))
            copies[-1].start()
    rate_copy.wait()
    set_decays(rate_buf[...], decay, decay8, decay16)

    def group_step(group, unused):
        at = lanes(group)
        product = key_buf[:, at].astype(F32) * value_buf[:, at].astype(F32)
        driven[:, at] = product
        blocks = [product[i:i + ROWS] for i in range(0, count, ROWS)]
        end_states(blocks, decay, decay8, decay16, turn.at[group % 2], other, at)
        return unused

    groups = size // LANES
    for i in range(chunks):
        copies[2 * i].wait()
        copies[2 * i + 1].wait()
        lax.fori_loop(i * groups, (i + 1) * groups, group_step, 0, unroll=groups)


def second_ends_kernel(x_ref, driven, rates, mine, decay, decay8, decay16, turn):
    count, width = driven.shape
    half = rates.shape[0] // 2
    set_decays(rates[pl.ds(pl.multiple_of(x_ref[0] * half, half), half), :], decay, decay8, decay16)

    def group_step(group, unused):
        at = lanes(group)
        blocks = [driven[i:i + ROWS, at] for i in range(0, count, ROWS)]
        end_states(blocks, decay, decay8, decay16, turn.at[group % 2], mine, at)
        return unused

    lax.fori_loop(0, width // LANES, group_step, 0, unroll=2)


def local_kernel(part, query, driven, rates, residues, skip, out, series, decays, scales):
    count = driven.shape[0]
    modes = rates.shape[0]

    def spread(i, unused):
        here = lanes(i)
        at = lanes(part * ROWS + i)
        for mode in range(0, modes, ROWS):
            rows = pl.ds(mode * ROWS + i, ROWS, stride=ROWS)
            decay = jnp.exp(-rates[mode:mode + ROWS, at])
            decays[rows, :] = decay
            scales[rows, :] = residues[mode:mode + ROWS, at] * jnp.sqrt(1.0 - decay * decay)
        for token in range(0, count, ROWS):
            series[pl.ds(token * ROWS + i, ROWS, stride=ROWS), :] = driven[token:token + ROWS, at]
        return unused

    lax.fori_loop(0, ROWS, spread, 0, unroll=2)
    decay = [decays[m * ROWS:(m + 1) * ROWS, :] for m in range(modes)]
    scale = [scales[m * ROWS:(m + 1) * ROWS, :] for m in range(modes)]

    def token_step(token, states):
        rows = pl.ds(pl.multiple_of(token * ROWS, ROWS), ROWS)
        now = series[rows, :]
        states = [s * d + now for s, d in zip(states, decay)]
        series[rows, :] = added(s * w for s, w in zip(states, scale))
        return states

    lax.fori_loop(0, count, token_step, [jnp.zeros((ROWS, LANES), F32)] * modes, unroll=8)

    def gate(i, unused):
        here = lanes(i)
        at = lanes(part * ROWS + i)
        gates = query[:, at].astype(F32)
        for token in range(0, count, ROWS):
            filtered = series[pl.ds(token * ROWS + i, ROWS, stride=ROWS), :]
            out[token:token + ROWS, here] = gates[token:token + ROWS] * (
                filtered + skip[:, at] * driven[token:token + ROWS, at]
            )
        return unused

    lax.fori_loop(0, ROWS, gate, 0, unroll=2)


def carry_kernel(which, pieces, final, x_ref, *refs):
    locals_, (query, carried, rates, scales, decays8), rest = refs[:pieces], refs[pieces:pieces + 5], refs[pieces + 5:]
    if final:
        gated, squares, decay, decay8, weights, turn, sums = rest
        sums[...] = jnp.zeros_like(sums)
    else:
        gated, decay, decay8, weights, turn = rest
    count, width = query.shape
    half = carried.shape[0]
    mine = x_ref[0] if which == 0 else 1 - x_ref[0]
    rows = pl.ds(pl.multiple_of(mine * half, half), half)
    rate = rates[rows, :]
    step = jnp.exp(-rate)
    decay[...] = step
    decay8[...] = decays8[rows, :]
    weights[...] = scales[rows, :] * carried[...]
    groups = width // LANES // pieces

    for piece, local in enumerate(locals_):
        def group_step(group, unused):
            here = lanes(group)
            at = lanes(piece * groups + group)
            slot = turn.at[group % 2]
            gates = query[:, at].astype(F32)
            term, factor = weights[:, at], decay[:, at]
            for token in range(ROWS):
                term = term * factor
                slot[pl.ds(token, half, stride=ROWS), :] = term
            terms = [slot[m * ROWS:(m + 1) * ROWS, :] for m in range(half)]
            factors = [spread_row(decay8, m, at) for m in range(half)]
            for i in range(0, count, ROWS):
                result = local[i:i + ROWS, here] + gates[i:i + ROWS] * added(terms)
                gated[i:i + ROWS, at] = result
                if final:
                    sums[i:i + ROWS, :] += result * result
                if i + ROWS < count:
                    terms = [t * f for t, f in zip(terms, factors)]
            return unused

        lax.fori_loop(0, groups, group_step, 0, unroll=4)
    if final:
        squares[...] = jnp.sum(jnp.transpose(sums[...]), axis=0, keepdims=True)


def scale_kernel(rates, residues, scales):
    decay = jnp.exp(-rates[...])
    scales[...] = residues[...] * jnp.sqrt(1.0 - decay * decay)


def decay_kernel(rates, decay8):
    decay8[...] = jnp.exp(-ROWS * rates[...])


def norm_kernel(parts, gated, gain, *rest):
    sums, (out, factors, buf, sems) = rest[:parts], rest[parts:]
    count, width = gated.shape
    factor = lax.rsqrt(added(part[...] for part in sums) / C + 1e-06)
    factors[...] = jnp.transpose(jnp.broadcast_to(factor, (LANES, count)))
    size = 4 * ROWS

    def copy(i):
        rows = pl.ds(pl.multiple_of(i * size, size), size)
        return pltpu.make_async_copy(buf.at[rows, :], out.at[rows, :], sems.at[i])

    def chunk_step(i, unused):
        rows = pl.ds(pl.multiple_of(i * size, size), size)
        factor = factors[rows, :]
        for group in range(width // LANES):
            at = slice(group * LANES, (group + 1) * LANES)
            buf[rows, at] = (gated[rows, at] * factor * gain[:, at]).astype(buf.dtype)
        copy(i).start()
        return unused

    lax.fori_loop(0, count // size, chunk_step, 0, unroll=count // size)
    for i in range(count // size):
        copy(i).wait()


def call(kernel, inputs, specs, outputs, out_specs=None, scratch=(), flops=0, name=None):
    size = sum(x.size * x.dtype.itemsize for x in (*inputs, *outputs))
    return pl.pallas_call(
        kernel,
        out_shape=outputs,
        in_specs=specs,
        out_specs=out_specs or [VMEM] * len(outputs),
        scratch_shapes=scratch,
        cost_estimate=pl.CostEstimate(flops=flops, bytes_accessed=size, transcendentals=0),
        compiler_params=pltpu.CompilerParams(vmem_limit_bytes=32 * 1024 * 1024),
        name=name,
    )(*inputs)


def body(ctx, tp, query, keys, values, rates, residues, skip, gain):
    count, width = keys.shape
    modes = rates.shape[0]
    half = modes // 2
    outer = ctx // 2
    f32 = lambda *shape: jax.ShapeDtypeStruct(shape, F32)
    vmem = lambda *shape: pltpu.VMEM(shape, F32)
    in_hbm = lambda x: pltpu.with_memory_space_constraint(x, pltpu.HBM)
    tied = lax.optimization_barrier
    own = lax.axis_index("ctx").astype(jnp.int32)
    z, x = own // 2, own % 2
    x_ref = x.reshape(1)
    work = 2 * half * count * width
    pair = [(i, i ^ 1) for i in range(ctx)]

    chunks = 4
    other, driven = call(
        lambda *refs: first_ends_kernel(chunks, *refs),
        (x_ref, in_hbm(keys), in_hbm(values), in_hbm(rates)),
        [SMEM, HBM, HBM, HBM],
        (f32(half, width), f32(count, width)),
        scratch=[
            pltpu.VMEM((count, width), keys.dtype),
            pltpu.VMEM((count, width), values.dtype),
            *[vmem(half, width)] * 4,
            vmem(2, half * ROWS, LANES),
            pltpu.SemaphoreType.DMA((2 * chunks + 1,)),
        ],
        flops=work,
        name="first_ends",
    )
    partner = lax.ppermute(other, "ctx", pair)
    (mine,) = call(
        second_ends_kernel,
        (x_ref, driven, rates),
        [SMEM, VMEM, VMEM],
        (f32(half, width),),
        scratch=[*[vmem(half, width)] * 3, vmem(2, half * ROWS, LANES)],
        flops=work,
        name="second_ends",
    )

    pieces = width // LANES // ROWS

    def local_part(part, driven):
        (local,) = call(
            lambda *refs: local_kernel(part, *refs),
            (query, driven, rates, residues, skip[None]),
            [VMEM] * 5,
            (f32(count, width // pieces),),
            scratch=[vmem(count * ROWS, LANES), vmem(modes * ROWS, LANES), vmem(modes * ROWS, LANES)],
            flops=4 * work // pieces,
            name="local_filter",
        )
        return local

    early = [local_part(part, driven) for part in range(pieces // 2)]
    partner, mine, early = tied((partner, mine, early))

    def shifted(array, by):
        return lax.ppermute(array, "ctx", [(i, (i + 2 * by) % ctx) for i in range(ctx)])

    my_rates = jnp.where(x == 0, rates[:half], rates[half:])
    step = jnp.exp(-my_rates * count)
    pair_state = jnp.where(x == 0, mine * step + partner, partner * step + mine)
    pair_state, driven = tied((pair_state, driven))

    def to_partner(before):
        return jnp.where(x == 0, before * step + mine, before)

    def late_parts():
        return [local_part(part, driven) for part in range(pieces // 2, pieces)]

    if outer == 4 and tp % 2 == 0:
        def moved(array, targets):
            def target(i, j):
                to = targets[i // 2]
                return (2 * to + i % 2) * tp + (j if to != i // 2 else j ^ 1)

            links = [(i * tp + j, target(i, j)) for i in range(ctx) for j in range(tp)]
            return lax.ppermute(array, ("ctx", "tp"), links)

        def traded(array, pairs):
            links = []
            for i in range(ctx):
                for j in range(tp):
                    links.append((i * tp + j, (i ^ 1) * tp + j if i // 2 in pairs else i * tp + (j ^ 1)))
            return lax.ppermute(array, ("ctx", "tp"), links)

        span = jnp.exp(-my_rates * (2 * count))
        pair_state, rates = tied((pair_state, rates))
        first_move = moved(pair_state, (1, 0, 2, 3))
        second_move = moved(pair_state, (2, 0, 3, 1))
        third_move = moved(pair_state, (0, 2, 1, 3))
        (scales,) = call(scale_kernel, (rates, residues), [VMEM] * 2, (f32(modes, width),), name="scales")
        first_move, scales = tied((first_move, scales))
        both = jnp.where(z == 1, span * first_move + pair_state, pair_state)
        handed = moved(both, (0, 3, 1, 2))
        sooner = to_partner(jnp.where(z == 1, first_move, 0.0))
        sooner, rates = tied((sooner, rates))
        got = traded(sooner, (0, 1))
        (decays8,) = call(decay_kernel, (rates,), [VMEM], (f32(modes, width),), flops=10**9, name="decays")
        handed, decays8 = tied((handed, decays8))
        before = jnp.where(
            z == 0,
            0.0,
            jnp.where(z == 1, first_move, jnp.where(z == 2, third_move + span * second_move, second_move + span * handed)),
        )
        received = jnp.where(z <= 1, got, traded(to_partner(before), (2, 3)))
    else:
        span = min(3, outer - 1)
        parts = [shifted(pair_state, by) for by in range(span, 0, -1)]
        (scales,) = call(scale_kernel, (rates, residues), [VMEM] * 2, (f32(modes, width),), name="scales")
        (decays8,) = call(decay_kernel, (rates,), [VMEM], (f32(modes, width),), flops=10**9, name="decays")
        before = jnp.zeros_like(mine)
        for by, states in zip(range(span, 0, -1), parts):
            weight = jnp.exp(-my_rates * (2 * count * (by - 1)))
            before = before + jnp.where(z >= by, weight * states, 0.0)
        while span < outer - 1:
            parts = [(by, shifted(before, by)) for by in range(3 * span, 0, -span) if by < outer]
            for by, states in parts:
                weight = jnp.exp(-my_rates * (2 * count * by))
                before = before + jnp.where(z >= by, weight * states, 0.0)
            span = 4 * span
        received = lax.ppermute(to_partner(before), "ctx", pair)

    before, driven = tied((before, driven))
    late = late_parts()
    kept = jnp.where(x == 0, before, before * step + partner)

    carry_scratch = [*[vmem(half, width)] * 3, vmem(2, half * ROWS, LANES)]
    locals_ = early + late
    (halfway,) = call(
        lambda *refs: carry_kernel(0, pieces, False, *refs),
        (x_ref, *locals_, query, kept, rates, scales, decays8),
        [SMEM] + [VMEM] * (pieces + 5),
        (f32(count, width),),
        scratch=carry_scratch,
        flops=work,
        name="add_kept",
    )
    gated, squares = call(
        lambda *refs: carry_kernel(1, 1, True, *refs),
        (x_ref, halfway, query, received, rates, scales, decays8),
        [SMEM] + [VMEM] * 6,
        (f32(count, width), f32(1, count)),
        scratch=[*carry_scratch, vmem(count, LANES)],
        flops=work,
        name="add_received",
    )

    parts = [squares]
    if tp & (tp - 1) == 0:
        mask = 1
        while mask < tp:
            parts = [added(parts)]
            parts.append(lax.ppermute(parts[0], "tp", [(i, i ^ mask) for i in range(tp)]))
            mask = 2 * mask + 1
    else:
        for by in range(1, tp):
            parts.append(lax.ppermute(squares, "tp", [(i, (i + by) % tp) for i in range(tp)]))
    (out,) = call(
        lambda *refs: norm_kernel(len(parts), *refs),
        (gated, gain[None], *parts),
        [VMEM] * (2 + len(parts)),
        (jax.ShapeDtypeStruct((count, width), query.dtype),),
        out_specs=[HBM],
        scratch=[
            vmem(count, LANES),
            pltpu.VMEM((count, width), query.dtype),
            pltpu.SemaphoreType.DMA((count // (4 * ROWS),)),
        ],
        flops=2 * count * width,
        name="norm",
    )
    return out


def solution(mesh):
    ctx, tp = mesh.shape["ctx"], mesh.shape["tp"]
    in_specs = (
        P("ctx", "tp"),
        P("ctx", "tp"),
        P("ctx", "tp"),
        P(None, "tp"),
        P(None, "tp"),
        P("tp"),
        P("tp"),
    )
    return jax.shard_map(
        lambda *arrays: body(ctx, tp, *arrays),
        mesh=mesh,
        in_specs=in_specs,
        out_specs=P("ctx", "tp"),
        check_vma=False,
    )
```

```python
import jax
import jax.numpy as jnp
from jax import lax
from jax.experimental import pallas as pl
from jax.experimental.pallas import tpu as pltpu
from jax.sharding import PartitionSpec as P

C = 8192
LANES = 128
ROWS = 8
F32 = jnp.float32
VMEM = pl.BlockSpec(memory_space=pltpu.VMEM)
SMEM = pl.BlockSpec(memory_space=pltpu.SMEM)
HBM = pl.BlockSpec(memory_space=pltpu.HBM)


def lanes(group):
    return pl.ds(pl.multiple_of(group * LANES, LANES), LANES)


def added(terms):
    terms = list(terms)
    while len(terms) > 1:
        odd = terms[len(terms) - len(terms) % 2:]
        terms = [a + b for a, b in zip(terms[::2], terms[1::2])] + odd
    return terms[0]


def spread_row(ref, row, at):
    return jnp.broadcast_to(ref[row:row + 1, at], (ROWS, LANES))


def end_states(blocks, decay, decay8, decay16, turn, out, at):
    modes = decay.shape[0]
    for mode in range(modes):
        factor = spread_row(decay16, mode, at)
        even, odd = blocks[0], blocks[1]
        for i in range(2, len(blocks), 2):
            even = even * factor + blocks[i]
            odd = odd * factor + blocks[i + 1]
        turn[mode * ROWS:(mode + 1) * ROWS, :] = even * spread_row(decay8, mode, at) + odd
    step = decay[:, at]
    state = turn[pl.ds(0, modes, stride=ROWS), :]
    for token in range(1, ROWS):
        state = state * step + turn[pl.ds(token, modes, stride=ROWS), :]
    out[:, at] = state


def set_decays(rate, decay, decay8, decay16):
    decay[...] = jnp.exp(-rate)
    decay8[...] = jnp.exp(-ROWS * rate)
    decay16[...] = jnp.exp(-2 * ROWS * rate)


def first_ends_kernel(chunks, x_ref, keys, values, rates, other, driven, key_buf, value_buf, rate_buf,
                      decay, decay8, decay16, turn, sems):
    count, width = key_buf.shape
    half = rate_buf.shape[0]
    size = width // chunks
    start = pl.multiple_of((1 - x_ref[0]) * half, half)
    rate_copy = pltpu.make_async_copy(rates.at[pl.ds(start, half), :], rate_buf, sems.at[2 * chunks])
    rate_copy.start()
    copies = []
    for i in range(chunks):
        at = pl.ds(i * size, size)
        for j, (source, target) in enumerate(((keys, key_buf), (values, value_buf))):
            copies.append(pltpu.make_async_copy(source.at[:, at], target.at[:, at], sems.at[2 * i + j]))
            copies[-1].start()
    rate_copy.wait()
    set_decays(rate_buf[...], decay, decay8, decay16)

    def group_step(group, unused):
        at = lanes(group)
        product = key_buf[:, at].astype(F32) * value_buf[:, at].astype(F32)
        driven[:, at] = product
        blocks = [product[i:i + ROWS] for i in range(0, count, ROWS)]
        end_states(blocks, decay, decay8, decay16, turn.at[group % 2], other, at)
        return unused

    groups = size // LANES
    for i in range(chunks):
        copies[2 * i].wait()
        copies[2 * i + 1].wait()
        lax.fori_loop(i * groups, (i + 1) * groups, group_step, 0, unroll=groups)


def second_ends_kernel(x_ref, driven, rates, mine, decay, decay8, decay16, turn):
    count, width = driven.shape
    half = rates.shape[0] // 2
    set_decays(rates[pl.ds(pl.multiple_of(x_ref[0] * half, half), half), :], decay, decay8, decay16)

    def group_step(group, unused):
        at = lanes(group)
        blocks = [driven[i:i + ROWS, at] for i in range(0, count, ROWS)]
        end_states(blocks, decay, decay8, decay16, turn.at[group % 2], mine, at)
        return unused

    lax.fori_loop(0, width // LANES, group_step, 0, unroll=2)


def local_kernel(part, query, driven, rates, residues, skip, out, series, decays, scales):
    count = driven.shape[0]
    modes = rates.shape[0]

    def spread(i, unused):
        here = lanes(i)
        at = lanes(part * ROWS + i)
        for mode in range(0, modes, ROWS):
            rows = pl.ds(mode * ROWS + i, ROWS, stride=ROWS)
            decay = jnp.exp(-rates[mode:mode + ROWS, at])
            decays[rows, :] = decay
            scales[rows, :] = residues[mode:mode + ROWS, at] * jnp.sqrt(1.0 - decay * decay)
        for token in range(0, count, ROWS):
            series[pl.ds(token * ROWS + i, ROWS, stride=ROWS), :] = driven[token:token + ROWS, at]
        return unused

    lax.fori_loop(0, ROWS, spread, 0, unroll=ROWS)
    decay = [decays[m * ROWS:(m + 1) * ROWS, :] for m in range(modes)]
    scale = [scales[m * ROWS:(m + 1) * ROWS, :] for m in range(modes)]

    def token_step(token, states):
        rows = pl.ds(pl.multiple_of(token * ROWS, ROWS), ROWS)
        now = series[rows, :]
        states = [s * d + now for s, d in zip(states, decay)]
        series[rows, :] = added(s * w for s, w in zip(states, scale))
        return states

    lax.fori_loop(0, count, token_step, [jnp.zeros((ROWS, LANES), F32)] * modes, unroll=8)

    def gate(i, unused):
        here = lanes(i)
        at = lanes(part * ROWS + i)
        gates = query[:, at].astype(F32)
        for token in range(0, count, ROWS):
            filtered = series[pl.ds(token * ROWS + i, ROWS, stride=ROWS), :]
            out[token:token + ROWS, here] = gates[token:token + ROWS] * (
                filtered + skip[:, at] * driven[token:token + ROWS, at]
            )
        return unused

    lax.fori_loop(0, ROWS, gate, 0, unroll=ROWS)


def carry_kernel(which, pieces, final, x_ref, *refs):
    locals_, (query, carried, rates, scales, decays8), rest = refs[:pieces], refs[pieces:pieces + 5], refs[pieces + 5:]
    if final:
        gated, squares, decay, decay8, weights, turn, sums = rest
        sums[...] = jnp.zeros_like(sums)
    else:
        gated, decay, decay8, weights, turn = rest
    count, width = query.shape
    half = carried.shape[0]
    mine = x_ref[0] if which == 0 else 1 - x_ref[0]
    rows = pl.ds(pl.multiple_of(mine * half, half), half)
    rate = rates[rows, :]
    step = jnp.exp(-rate)
    decay[...] = step
    decay8[...] = decays8[rows, :]
    weights[...] = scales[rows, :] * carried[...]
    groups = width // LANES // pieces

    for piece, local in enumerate(locals_):
        def group_step(group, unused):
            here = lanes(group)
            at = lanes(piece * groups + group)
            slot = turn.at[group % 2]
            gates = query[:, at].astype(F32)
            term, factor = weights[:, at], decay[:, at]
            for token in range(ROWS):
                term = term * factor
                slot[pl.ds(token, half, stride=ROWS), :] = term
            terms = [slot[m * ROWS:(m + 1) * ROWS, :] for m in range(half)]
            factors = [spread_row(decay8, m, at) for m in range(half)]
            for i in range(0, count, ROWS):
                result = local[i:i + ROWS, here] + gates[i:i + ROWS] * added(terms)
                gated[i:i + ROWS, at] = result
                if final:
                    sums[i:i + ROWS, :] += result * result
                if i + ROWS < count:
                    terms = [t * f for t, f in zip(terms, factors)]
            return unused

        lax.fori_loop(0, groups, group_step, 0, unroll=groups)
    if final:
        squares[...] = jnp.sum(jnp.transpose(sums[...]), axis=0, keepdims=True)


def scale_kernel(rates, residues, scales):
    decay = jnp.exp(-rates[...])
    scales[...] = residues[...] * jnp.sqrt(1.0 - decay * decay)


def decay_kernel(rates, decay8):
    decay8[...] = jnp.exp(-ROWS * rates[...])


def norm_kernel(parts, gated, gain, *rest):
    sums, (out, factors, buf, sems) = rest[:parts], rest[parts:]
    count, width = gated.shape
    factor = lax.rsqrt(added(part[...] for part in sums) / C + 1e-06)
    factors[...] = jnp.transpose(jnp.broadcast_to(factor, (LANES, count)))
    size = 4 * ROWS

    def copy(i):
        rows = pl.ds(pl.multiple_of(i * size, size), size)
        return pltpu.make_async_copy(buf.at[rows, :], out.at[rows, :], sems.at[i])

    def chunk_step(i, unused):
        rows = pl.ds(pl.multiple_of(i * size, size), size)
        factor = factors[rows, :]
        for group in range(width // LANES):
            at = slice(group * LANES, (group + 1) * LANES)
            buf[rows, at] = (gated[rows, at] * factor * gain[:, at]).astype(buf.dtype)
        copy(i).start()
        return unused

    lax.fori_loop(0, count // size, chunk_step, 0, unroll=count // size)
    for i in range(count // size):
        copy(i).wait()


def call(kernel, inputs, specs, outputs, out_specs=None, scratch=(), flops=0, name=None):
    size = sum(x.size * x.dtype.itemsize for x in (*inputs, *outputs))
    return pl.pallas_call(
        kernel,
        out_shape=outputs,
        in_specs=specs,
        out_specs=out_specs or [VMEM] * len(outputs),
        scratch_shapes=scratch,
        cost_estimate=pl.CostEstimate(flops=flops, bytes_accessed=size, transcendentals=0),
        compiler_params=pltpu.CompilerParams(vmem_limit_bytes=32 * 1024 * 1024),
        name=name,
    )(*inputs)


def body(ctx, tp, query, keys, values, rates, residues, skip, gain):
    count, width = keys.shape
    modes = rates.shape[0]
    half = modes // 2
    outer = ctx // 2
    f32 = lambda *shape: jax.ShapeDtypeStruct(shape, F32)
    vmem = lambda *shape: pltpu.VMEM(shape, F32)
    in_hbm = lambda x: pltpu.with_memory_space_constraint(x, pltpu.HBM)
    tied = lax.optimization_barrier
    own = lax.axis_index("ctx").astype(jnp.int32)
    z, x = own // 2, own % 2
    x_ref = x.reshape(1)
    work = 2 * half * count * width
    pair = [(i, i ^ 1) for i in range(ctx)]

    chunks = 4
    other, driven = call(
        lambda *refs: first_ends_kernel(chunks, *refs),
        (x_ref, in_hbm(keys), in_hbm(values), in_hbm(rates)),
        [SMEM, HBM, HBM, HBM],
        (f32(half, width), f32(count, width)),
        scratch=[
            pltpu.VMEM((count, width), keys.dtype),
            pltpu.VMEM((count, width), values.dtype),
            *[vmem(half, width)] * 4,
            vmem(2, half * ROWS, LANES),
            pltpu.SemaphoreType.DMA((2 * chunks + 1,)),
        ],
        flops=work,
        name="first_ends",
    )
    partner = lax.ppermute(other, "ctx", pair)
    (mine,) = call(
        second_ends_kernel,
        (x_ref, driven, rates),
        [SMEM, VMEM, VMEM],
        (f32(half, width),),
        scratch=[*[vmem(half, width)] * 3, vmem(2, half * ROWS, LANES)],
        flops=work,
        name="second_ends",
    )

    pieces = width // LANES // ROWS

    def local_part(part, driven):
        (local,) = call(
            lambda *refs: local_kernel(part, *refs),
            (query, driven, rates, residues, skip[None]),
            [VMEM] * 5,
            (f32(count, width // pieces),),
            scratch=[vmem(count * ROWS, LANES), vmem(modes * ROWS, LANES), vmem(modes * ROWS, LANES)],
            flops=4 * work // pieces,
            name="local_filter",
        )
        return local

    early = [local_part(part, driven) for part in range(pieces // 2)]
    partner, mine, early = tied((partner, mine, early))

    def shifted(array, by):
        return lax.ppermute(array, "ctx", [(i, (i + 2 * by) % ctx) for i in range(ctx)])

    my_rates = jnp.where(x == 0, rates[:half], rates[half:])
    step = jnp.exp(-my_rates * count)
    pair_state = jnp.where(x == 0, mine * step + partner, partner * step + mine)
    pair_state, driven = tied((pair_state, driven))

    def to_partner(before):
        return jnp.where(x == 0, before * step + mine, before)

    def late_parts():
        return [local_part(part, driven) for part in range(pieces // 2, pieces)]

    if outer == 4 and tp % 2 == 0:
        def moved(array, targets):
            def target(i, j):
                to = targets[i // 2]
                return (2 * to + i % 2) * tp + (j if to != i // 2 else j ^ 1)

            links = [(i * tp + j, target(i, j)) for i in range(ctx) for j in range(tp)]
            return lax.ppermute(array, ("ctx", "tp"), links)

        def traded(array, pairs):
            links = []
            for i in range(ctx):
                for j in range(tp):
                    links.append((i * tp + j, (i ^ 1) * tp + j if i // 2 in pairs else i * tp + (j ^ 1)))
            return lax.ppermute(array, ("ctx", "tp"), links)

        span = jnp.exp(-my_rates * (2 * count))
        pair_state, rates = tied((pair_state, rates))
        first_move = moved(pair_state, (1, 0, 2, 3))
        second_move = moved(pair_state, (2, 0, 3, 1))
        third_move = moved(pair_state, (0, 2, 1, 3))
        (scales,) = call(scale_kernel, (rates, residues), [VMEM] * 2, (f32(modes, width),), name="scales")
        first_move, scales = tied((first_move, scales))
        both = jnp.where(z == 1, span * first_move + pair_state, pair_state)
        handed = moved(both, (0, 3, 1, 2))
        sooner = to_partner(jnp.where(z == 1, first_move, 0.0))
        sooner, rates = tied((sooner, rates))
        got = traded(sooner, (0, 1))
        (decays8,) = call(decay_kernel, (rates,), [VMEM], (f32(modes, width),), flops=10**9, name="decays")
        handed, decays8 = tied((handed, decays8))
        before = jnp.where(
            z == 0,
            0.0,
            jnp.where(z == 1, first_move, jnp.where(z == 2, third_move + span * second_move, second_move + span * handed)),
        )
        received = jnp.where(z <= 1, got, traded(to_partner(before), (2, 3)))
    else:
        span = min(3, outer - 1)
        parts = [shifted(pair_state, by) for by in range(span, 0, -1)]
        (scales,) = call(scale_kernel, (rates, residues), [VMEM] * 2, (f32(modes, width),), name="scales")
        (decays8,) = call(decay_kernel, (rates,), [VMEM], (f32(modes, width),), flops=10**9, name="decays")
        before = jnp.zeros_like(mine)
        for by, states in zip(range(span, 0, -1), parts):
            weight = jnp.exp(-my_rates * (2 * count * (by - 1)))
            before = before + jnp.where(z >= by, weight * states, 0.0)
        while span < outer - 1:
            parts = [(by, shifted(before, by)) for by in range(3 * span, 0, -span) if by < outer]
            for by, states in parts:
                weight = jnp.exp(-my_rates * (2 * count * by))
                before = before + jnp.where(z >= by, weight * states, 0.0)
            span = 4 * span
        received = lax.ppermute(to_partner(before), "ctx", pair)

    before, driven = tied((before, driven))
    late = late_parts()
    kept = jnp.where(x == 0, before, before * step + partner)

    carry_scratch = [*[vmem(half, width)] * 3, vmem(2, half * ROWS, LANES)]
    locals_ = early + late
    (halfway,) = call(
        lambda *refs: carry_kernel(0, pieces, False, *refs),
        (x_ref, *locals_, query, kept, rates, scales, decays8),
        [SMEM] + [VMEM] * (pieces + 5),
        (f32(count, width),),
        scratch=carry_scratch,
        flops=work,
        name="add_kept",
    )
    gated, squares = call(
        lambda *refs: carry_kernel(1, 1, True, *refs),
        (x_ref, halfway, query, received, rates, scales, decays8),
        [SMEM] + [VMEM] * 6,
        (f32(count, width), f32(1, count)),
        scratch=[*carry_scratch, vmem(count, LANES)],
        flops=work,
        name="add_received",
    )

    parts = [squares]
    if tp & (tp - 1) == 0:
        mask = 1
        while mask < tp:
            parts = [added(parts)]
            parts.append(lax.ppermute(parts[0], "tp", [(i, i ^ mask) for i in range(tp)]))
            mask = 2 * mask + 1
    else:
        for by in range(1, tp):
            parts.append(lax.ppermute(squares, "tp", [(i, (i + by) % tp) for i in range(tp)]))
    (out,) = call(
        lambda *refs: norm_kernel(len(parts), *refs),
        (gated, gain[None], *parts),
        [VMEM] * (2 + len(parts)),
        (jax.ShapeDtypeStruct((count, width), query.dtype),),
        out_specs=[HBM],
        scratch=[
            vmem(count, LANES),
            pltpu.VMEM((count, width), query.dtype),
            pltpu.SemaphoreType.DMA((count // (4 * ROWS),)),
        ],
        flops=2 * count * width,
        name="norm",
    )
    return out


def solution(mesh):
    ctx, tp = mesh.shape["ctx"], mesh.shape["tp"]
    in_specs = (
        P("ctx", "tp"),
        P("ctx", "tp"),
        P("ctx", "tp"),
        P(None, "tp"),
        P(None, "tp"),
        P("tp"),
        P("tp"),
    )
    return jax.shard_map(
        lambda *arrays: body(ctx, tp, *arrays),
        mesh=mesh,
        in_specs=in_specs,
        out_specs=P("ctx", "tp"),
        check_vma=False,
    )
```
